128 devices in a mesh: scen: 8 (over x, z_hi), crow: 4 (over z_lo, core), ccol: 4 (over y).
Axes of the slice: x: 4, y: 4, z: 4 (z_hi: 2, z_lo: 2; z = z_hi * 2 + z_lo), core: 2. Of those that a mesh axis runs over, the one named last changes fastest.
Arguments:
- kkt: float32 [512, 512, 512], P(('scen', 'crow', 'ccol')), as said below
- border: bfloat16 [512, 512, 512], P(('scen', 'crow', 'ccol')), may hold values from -0.25 to 0.25
- linked: int32 [512, 512], P(('scen', 'crow', 'ccol')), may hold values from 0 to 8191, as said below
- rhs_second: float32 [512, 512], P(('scen', 'crow', 'ccol')), may hold values from -6 to 6
- rhs_first: float32 [512], replicated, may hold values from -360 to 360
- first_diag: float32 [512], replicated, may hold values from 1 to 10
Outputs:
- panel_factor: float32 [8192, 512], P('crow', 'ccol')
- first_step: float32 [512], replicated
- second_step: float32 [512, 512], P(('scen', 'crow', 'ccol'))
The draws below stay inside these ranges and needn't reach their ends.
Inputs may be any that keep to these rules, and one draw needn't show every extreme that they name: `linked`: each scenario's row holds 512 distinct first-section columns, of which exactly 256 lie below 512. `kkt`: each block is symmetric and strictly diagonally dominant with a positive diagonal.
All inputs are finite; a program needn't handle non-finite values.
Results may differ from the reference program's by a relative error of at most 0.0003.
Values sent between devices are 32-bit elements; how exact they have to be, the bound alone decides.
A program may use at most 128 MiB of HBM per device.

```python
import math
import jax
import jax.numpy as jnp
from jax import lax

KKT = 512
LINKS = 512
FIRST = 8192
PANEL = 512
SCENARIOS = 512


def draw_kkt(key, part):
    key = jax.random.fold_in(key, 11)
    key_band, key_noise, key_scale, key_margin = jax.random.split(key, 4)
    scale_top = 2.0
    margin_low = 0.002
    margin_top = 0.02
    band_width = min(8, KKT // 2)
    positions = jnp.arange(KKT, dtype=jnp.int32)
    apart = jnp.abs(positions[:, None] - positions[None, :])
    in_band = ((apart >= 1) & (apart <= band_width)).astype(jnp.float32)
    identity = jnp.eye(KKT, dtype=jnp.float32)
    band = jax.random.uniform(key_band, (SCENARIOS, KKT, KKT), jnp.float32, 0.5, 1.0)
    band = -0.5 * (band + jnp.swapaxes(band, 1, 2)) * in_band * (8.0 / (1.5 * band_width))
    noise = jax.random.uniform(key_noise, (SCENARIOS, KKT, KKT), jnp.float32, -1.0, 1.0)
    noise = 0.5 * (noise + jnp.swapaxes(noise, 1, 2)) * (1.0 - identity) * (0.12 / KKT)
    row_scale = jnp.exp(jax.random.uniform(key_scale, (SCENARIOS, KKT), jnp.float32, 0.0, math.log(scale_top)))
    offdiag = row_scale[:, :, None] * row_scale[:, None, :] * (band + noise)
    margin = jax.random.uniform(key_margin, (SCENARIOS, KKT), jnp.float32, margin_low, margin_top)
    diagonal = (1.0 + margin) * jnp.sum(jnp.abs(offdiag), axis=2)
    return offdiag + diagonal[:, :, None] * identity


def draw_linked(key, part):
    key = jax.random.fold_in(key, 23)
    keys = jax.random.split(key, SCENARIOS)
    inside = LINKS // 2
    outside = LINKS - inside

    def one_row(row_key):
        key_low, key_high, key_order = jax.random.split(row_key, 3)
        low = jax.random.permutation(key_low, PANEL)[:inside]
        high = PANEL + jax.random.permutation(key_high, FIRST - PANEL)[:outside]
        both = jnp.concatenate([low, high]).astype(jnp.int32)
        return jax.random.permutation(key_order, both).astype(jnp.int32)
    return jax.vmap(one_row)(keys)


def steps_of(stream_key, dims, pieces, smallest, top_value):
    loudness, own = 1.0, jax.random.fold_in(stream_key, 6)
    for dim, parts in pieces:
        draws = jnp.exp(jax.random.uniform(jax.random.fold_in(own, dim), (parts,), jnp.float32, smallest / len(pieces), top_value / len(pieces)))
        loudness = loudness * jnp.repeat(draws, dims[dim] // parts).reshape([-1 if axis == dim else 1 for axis in range(len(dims))])
    return loudness


def scatter_about(stream_key, shape, scale, limit, cuts=(), kind=jnp.bfloat16):
    result = scale * jax.random.normal(stream_key, shape, jnp.float32)
    if cuts:
        result = result * steps_of(stream_key, shape, cuts, -0.22, 0.18)
    return jnp.clip(result, -limit, limit).astype(kind)


def setup_inputs(seed: int = 0) -> dict:
    key_of = jax.random.split(jax.random.key(seed), 7)
    kkt = draw_kkt(jax.random.fold_in(key_of[6], 71), 0)
    border = scatter_about(key_of[1], (SCENARIOS, KKT, LINKS), KKT ** -0.5, 0.25, ((0, 128),))
    linked = draw_linked(jax.random.fold_in(key_of[6], 71), 0)
    rhs_second = scatter_about(key_of[3], (SCENARIOS, KKT), 1.0, 6.0, ((0, 128),), jnp.float32)
    rhs_first = scatter_about(key_of[4], (PANEL,), 60.0, 360.0, (), jnp.float32)
    first_diag = jnp.clip(jnp.exp(jax.random.uniform(key_of[5], (PANEL,), jnp.float32, math.log(1.0), math.log(10.0))), 1.0, 10.0)
    return {"kkt": kkt, "border": border, "linked": linked, "rhs_second": rhs_second, "rhs_first": rhs_first, "first_diag": first_diag}


def cho_apply(factor, rhs):
    half = lax.linalg.triangular_solve(factor, rhs, left_side=True, lower=True)
    return lax.linalg.triangular_solve(factor, half, left_side=True, lower=True, transpose_a=True)

def scenario_parts(kkt_one, border_one, linked_one):
    factor = jnp.linalg.cholesky(kkt_one)
    select = (linked_one[:, None] == jnp.arange(PANEL, dtype=jnp.int32)[None, :]).astype(jnp.bfloat16)
    placed = jnp.dot(border_one.astype(jnp.float32), select.astype(jnp.float32), preferred_element_type=jnp.float32)
    solved = cho_apply(factor, placed)
    coupling = jnp.dot(border_one.astype(jnp.float32).T, solved, precision=lax.Precision.HIGHEST)
    return (factor, placed, coupling)

def reference(kkt, border, linked, rhs_second, rhs_first, first_diag):

    def accumulate(schur, items):
        kkt_one, border_one, linked_one = items
        factor, placed, coupling = scenario_parts(kkt_one, border_one, linked_one)
        return (schur.at[linked_one].add(coupling), None)
    schur, unused = lax.scan(accumulate, jnp.zeros((FIRST, PANEL), jnp.float32), (kkt, border, linked))
    head = schur[:PANEL] + jnp.diag(first_diag)
    lead = jnp.linalg.cholesky(head)
    lead_inv = lax.linalg.triangular_solve(lead, jnp.eye(PANEL, dtype=jnp.float32), left_side=True, lower=True)
    lower = jnp.dot(schur, lead_inv.T, precision=lax.Precision.HIGHEST)
    top = jnp.pad(lead, ((0, FIRST - PANEL), (0, 0)))
    rows_index = jnp.arange(FIRST, dtype=jnp.int32)[:, None]
    panel_factor = jnp.where(rows_index < PANEL, top, lower)
    inner = jnp.dot(lead_inv, rhs_first, precision=lax.Precision.HIGHEST)
    first_step = jnp.dot(lead_inv.T, inner, precision=lax.Precision.HIGHEST)

    def second(items):
        kkt_one, border_one, linked_one, rhs_one = items
        factor, placed, coupling = scenario_parts(kkt_one, border_one, linked_one)
        moved = rhs_one - jnp.dot(placed, first_step, precision=lax.Precision.HIGHEST)
        return cho_apply(factor, moved[:, None])[:, 0]
    second_step = lax.map(second, (kkt, border, linked, rhs_second))
    return (panel_factor, first_step, second_step)
```

```python
import jax
import jax.numpy as jnp
from jax import lax
from jax.experimental import pallas as pl
from jax.experimental.pallas import tpu as pltpu
from jax.sharding import PartitionSpec as P

F32 = jnp.float32
BF16 = jnp.bfloat16
B = 128
FIRST = 8192
INSIDE = 256


def split2(x):
    hi = x.astype(BF16)
    lo = (x - hi.astype(F32)).astype(BF16)
    return hi, lo


def dot_t(x, y):
    xh, xl = split2(x)
    yh, yl = split2(y)
    return lax.dot_general(
        jnp.concatenate([xh, xh, xl], axis=0),
        jnp.concatenate([yh, yl, yh], axis=0),
        (((0,), (0,)), ((), ())),
        preferred_element_type=F32,
    )


def dot_n(x, y):
    xh, xl = split2(x)
    yh, yl = split2(y)
    return lax.dot_general(
        jnp.concatenate([xh, xh, xl], axis=1),
        jnp.concatenate([yh, yl, yh], axis=0),
        (((1,), (0,)), ((), ())),
        preferred_element_type=F32,
    )


def pieces3(x):
    h = x.astype(BF16).astype(F32)
    r = x - h
    m = r.astype(BF16).astype(F32)
    return h, m, r - m


def rank8(x, y):
    xh, xm, xl = pieces3(x)
    yh, ym, yl = pieces3(y)
    return lax.dot_general(
        jnp.concatenate([xh, xh, xm, xm, xh, xl], axis=0).astype(BF16),
        jnp.concatenate([yh, ym, yh, ym, yl, yh], axis=0).astype(BF16),
        (((0,), (0,)), ((), ())),
        preferred_element_type=F32,
    )


def eliminate_block(blk):
    S = blk.shape[0]
    lane = lax.broadcasted_iota(jnp.int32, (1, 8, B), 2)
    row = lax.broadcasted_iota(jnp.int32, (1, 8, B), 1)
    for t in range(B // 8):
        k0 = 8 * t
        p = blk[:, k0 : k0 + 8, :]
        cols = [jnp.broadcast_to(p[:, :, k0 + m : k0 + m + 1], (S, 8, B)) for m in range(8)]
        scale = jnp.zeros((S, 8, B), F32)
        for j in range(8):
            d = cols[j][:, j : j + 1, :]
            rd = jnp.broadcast_to(1.0 / d, (S, 8, B))
            scale = jnp.where(row == j, rd, scale)
            if j < 7:
                mult = jnp.where(row > j, cols[j] * rd, 0.0)
                prow = jnp.where(lane[:, :1] == k0 + j, 1.0, p[:, j : j + 1, :])
                p = jnp.where((lane == k0 + j) & (row > j), 0.0, p) - mult * prow
                for m in range(j + 1, 8):
                    cols[m] = cols[m] - mult * cols[m][:, j : j + 1, :]
        blk[:, k0 : k0 + 8, :] = p
        if t < B // 8 - 1:
            off = lane - k0
            scaled = p * scale
            aug = jnp.where((off > row) & (off < 8), 0.0, jnp.where(off == row, 1.0, p))
            inblk = (lane >= k0) & (lane < k0 + 8)
            r0 = k0 + 8
            for s in range(S):
                upd = rank8(scaled[s], aug[s])
                blk[s, r0:, :] = jnp.where(inblk[0, :1], 0.0, blk[s, r0:, :]) - upd[r0:, :]


def factor(work, blk, tri, steps):
    S = work.shape[0]
    r_i = lax.broadcasted_iota(jnp.int32, (B, B), 0)
    c_i = lax.broadcasted_iota(jnp.int32, (B, B), 1)

    def body(j, _):
        rows = pl.ds(pl.multiple_of(j * B, B), B)
        blk[...] = work[:, rows, rows]
        eliminate_block(blk)
        for s in range(S):
            a = blk[s]
            d = jnp.sum(jnp.where(r_i == c_i, a, 0.0), axis=1, keepdims=True)
            t = jnp.where(c_i < r_i, a, jnp.where(c_i == r_i, 1.0, 0.0)) * lax.rsqrt(d)
            tri[s, j] = t
            work[s, rows, :] = dot_n(t, work[s, rows, :])

            def update(i, _, s=s):
                rows_i = pl.ds(pl.multiple_of(i * B, B), B)
                work[s, rows_i, :] -= dot_t(work[s, rows, rows_i], work[s, rows, :])
                return 0

            lax.fori_loop(j + 1, steps, update, 0)
        return 0

    lax.fori_loop(0, steps, body, 0)


def scenario_kernel(kkt, border, lcol, lrow, rcol, head, y, ids, work, tri, blk):
    S, n, _ = kkt.shape
    panel = head.shape[0]
    half = y.shape[2]
    cols = y.shape[3]
    lanes = lax.broadcasted_iota(jnp.int32, (n, panel + half), 1)
    first_lane = lax.broadcasted_iota(jnp.int32, (n, B), 1) == 0
    for s in range(S):
        own = lcol[s]
        before = jnp.where(lrow[s : s + 1, :] < own, 1.0, 0.0)
        rank = jnp.sum(before, axis=1, keepdims=True).astype(jnp.int32)
        place = jnp.where(own < panel, own, panel + rank - (n - half))
        hot = jnp.where(lanes == place, 1.0, 0.0)
        ids[s : s + 1, :] = jnp.sum(
            jnp.where(lanes[:, panel:] == place, own, 0), axis=0, keepdims=True
        )
        work[s, :, :n] = kkt[s]
        work[s, :, n : n + panel + half] = jnp.dot(
            border[s], hot.astype(BF16), preferred_element_type=F32
        )
        work[s, :, n + panel + half :] = jnp.where(first_lane, rcol[s], 0.0)
    factor(work, blk, tri, n // B)
    total = None
    for s in range(S):
        wp = work[s, :, n : n + panel]
        wo = work[s, :, n + panel : n + panel + half]
        part = dot_t(wp, wp)
        total = part if total is None else total + part
        out = dot_t(wo, wp)
        for c in range(panel // cols):
            y[c, s] = out[:, c * cols : (c + 1) * cols]
    head[...] = total


def scatter_kernel(ids, y, dense):
    dense[...] = jnp.zeros_like(dense)
    groups, half, _ = y.shape

    def body(i, _):
        s = i // (half // 8)
        r0 = pl.multiple_of(lax.rem(i, half // 8) * 8, 8)
        where = [ids[s, r0 + k] for k in range(8)]
        tile = y[s, pl.ds(r0, 8), :]
        old = [dense[pl.ds(where[k], 1), :] for k in range(8)]
        for k in range(8):
            dense[pl.ds(where[k], 1), :] = old[k] + tile[k : k + 1, :]
        return 0

    lax.fori_loop(0, groups * half // 8, body, 0)


def head_kernel(head, diag, rhs, lead_t, lead_inv, step, work, tri, blk):
    n = head.shape[0]
    r_i = lax.broadcasted_iota(jnp.int32, (n, n), 0)
    c_i = lax.broadcasted_iota(jnp.int32, (n, n), 1)
    first_lane = lax.broadcasted_iota(jnp.int32, (n, B), 1) == 0
    work[0, :, :n] = head[...] + jnp.where(r_i == c_i, diag[...], 0.0)
    work[0, :, n : 2 * n] = jnp.where(r_i == c_i, 1.0, 0.0)
    work[0, :, 2 * n :] = jnp.where(first_lane, rhs[...], 0.0)
    factor(work, blk, tri, n // B)
    lead_t[...] = jnp.where(c_i >= r_i, work[0, :, :n], 0.0)
    inv = work[0, :, n : 2 * n]
    lead_inv[...] = inv
    step[...] = jnp.sum(inv * work[0, :, 2 * n : 2 * n + 1], axis=0, keepdims=True)


def panel_kernel(rows, lead_inv, lead_t, out):
    panel = lead_t.shape[0]
    cols = out.shape[1]
    at = pl.ds(pl.multiple_of(lax.axis_index("ccol") * cols, cols), cols)
    ih, il = split2(lead_inv[at, :])
    own = jnp.concatenate([ih, il, ih], axis=1)
    step = 512
    for r in range(rows.shape[0] // step):
        rh, rl = split2(rows[r * step : (r + 1) * step, :])
        out[r * step : (r + 1) * step, :] = lax.dot_general(
            jnp.concatenate([rh, rh, rl], axis=1),
            own,
            (((1,), (1,)), ((), ())),
            preferred_element_type=F32,
        )

    @pl.when(lax.axis_index("crow") == 0)
    def _():
        out[:panel, :] = lead_t[at, :].T


def second_kernel(work, tri, step, out):
    S, n, _ = work.shape
    panel = step.shape[1]
    f = step[...]
    for s in range(S):
        moved = work[s, :, n + panel + panel // 2 : n + panel + panel // 2 + 1] - jnp.sum(
            work[s, :, n : n + panel] * f, axis=1, keepdims=True
        )
        x = [None] * (n // B)
        for j in reversed(range(n // B)):
            rows = slice(j * B, (j + 1) * B)
            left = moved[rows]
            for i in range(j + 1, n // B):
                left = left - jnp.sum(
                    work[s, rows, i * B : (i + 1) * B] * x[i], axis=1, keepdims=True
                )
            x[j] = jnp.sum(tri[s, j] * left, axis=0, keepdims=True)
            out[s : s + 1, j * B : (j + 1) * B] = x[j]


VMEM = pl.BlockSpec(memory_space=pltpu.VMEM)
SMEM = pl.BlockSpec(memory_space=pltpu.SMEM)
LIMIT = 60 * 2**20


def local_call(kernel, outs, in_specs, scratch=(), flops=0):
    return pl.pallas_call(
        kernel,
        out_shape=outs,
        in_specs=in_specs,
        out_specs=tuple(VMEM for _ in outs) if isinstance(outs, tuple) else VMEM,
        scratch_shapes=list(scratch),
        compiler_params=pltpu.CompilerParams(vmem_limit_bytes=LIMIT),
        cost_estimate=pl.CostEstimate(flops=flops, bytes_accessed=2**20, transcendentals=0),
    )


def shape(*dims, dtype=F32):
    return jax.ShapeDtypeStruct(dims, dtype)


def per_device(kkt, border, linked, rhs_second, rhs_first, first_diag):
    S, n, _ = kkt.shape
    panel = rhs_first.shape[0]
    num_rows = lax.axis_size("crow")
    num_cols = lax.axis_size("ccol")
    tile_rows = FIRST // num_rows
    cols = panel // num_cols
    half = n - INSIDE
    width = n + panel + half + B
    head, y, ids, work, tri = local_call(
        scenario_kernel,
        (
            shape(panel, panel),
            shape(num_cols, S, half, cols),
            shape(S, half, dtype=jnp.int32),
            shape(S, n, width),
            shape(S, n // B, B, B),
        ),
        [VMEM] * 5,
        [pltpu.VMEM((S, B, B), F32)],
        flops=40 * 10**9,
    )(kkt, border, linked[:, :, None], linked, rhs_second[:, :, None])
    ids = lax.all_gather(ids, "ccol", axis=0, tiled=True)
    y = lax.all_to_all(y, "ccol", 0, 0)
    head = lax.psum(head, ("scen", "crow", "ccol"))
    dense = local_call(scatter_kernel, shape(FIRST, cols), [SMEM, VMEM])(
        ids, y.reshape(num_cols * S, half, cols)
    )
    tile = lax.psum(lax.psum_scatter(dense, "crow", scatter_dimension=0, tiled=True), "scen")
    rows = lax.all_gather(tile, "ccol", axis=1, tiled=True)
    lead_t, lead_inv, step = local_call(
        head_kernel,
        (shape(panel, panel), shape(panel, panel), shape(1, panel)),
        [VMEM] * 3,
        [
            pltpu.VMEM((1, panel, 2 * panel + B), F32),
            pltpu.VMEM((1, panel // B, B, B), F32),
            pltpu.VMEM((1, B, B), F32),
        ],
        flops=40 * 10**9,
    )(head, first_diag[None, :], rhs_first[:, None])
    panel_factor = local_call(panel_kernel, shape(tile_rows, cols), [VMEM] * 3)(
        rows, lead_inv, lead_t
    )
    second = local_call(second_kernel, shape(S, n), [VMEM] * 3)(work, tri, step)
    return (panel_factor, step[0], second)


def solution(mesh):
    placed = (
        P(("scen", "crow", "ccol"), None, None),
        P(("scen", "crow", "ccol"), None, None),
        P(("scen", "crow", "ccol"), None),
        P(("scen", "crow", "ccol"), None),
        P(),
        P(),
    )
    return jax.shard_map(
        per_device,
        mesh=mesh,
        in_specs=placed,
        out_specs=(P("crow", "ccol"), P(), P(("scen", "crow", "ccol"), None)),
        check_vma=False,
    )
```

```python
import jax
import jax.numpy as jnp
from jax import lax
from jax.experimental import pallas as pl
from jax.experimental.pallas import tpu as pltpu
from jax.sharding import PartitionSpec as P

F32 = jnp.float32
BF16 = jnp.bfloat16
B = 128
FIRST = 8192
INSIDE = 256


def split2(x):
    hi = x.astype(BF16)
    lo = (x - hi.astype(F32)).astype(BF16)
    return hi, lo


def dot_t(x, y):
    xh, xl = split2(x)
    yh, yl = split2(y)
    return lax.dot_general(
        jnp.concatenate([xh, xh, xl], axis=0),
        jnp.concatenate([yh, yl, yh], axis=0),
        (((0,), (0,)), ((), ())),
        preferred_element_type=F32,
    )


def dot_n(x, y):
    xh, xl = split2(x)
    yh, yl = split2(y)
    return lax.dot_general(
        jnp.concatenate([xh, xh, xl], axis=1),
        jnp.concatenate([yh, yl, yh], axis=0),
        (((1,), (0,)), ((), ())),
        preferred_element_type=F32,
    )


def dot_nt(x, y):
    xh, xl = split2(x)
    yh, yl = split2(y)
    return lax.dot_general(
        jnp.concatenate([xh, xh, xl], axis=1),
        jnp.concatenate([yh, yl, yh], axis=1),
        (((1,), (1,)), ((), ())),
        preferred_element_type=F32,
    )


def pieces3(x):
    h = x.astype(BF16).astype(F32)
    r = x - h
    m = r.astype(BF16).astype(F32)
    return h, m, r - m


def rank8(x, y):
    xh, xm, xl = pieces3(x)
    yh, ym, yl = pieces3(y)
    return lax.dot_general(
        jnp.concatenate([xh, xh, xm, xm, xh, xl], axis=0).astype(BF16),
        jnp.concatenate([yh, ym, yh, ym, yl, yh], axis=0).astype(BF16),
        (((0,), (0,)), ((), ())),
        preferred_element_type=F32,
    )


def eliminate_block(blk):
    S = blk.shape[0]
    lane = lax.broadcasted_iota(jnp.int32, (1, 8, B), 2)
    row = lax.broadcasted_iota(jnp.int32, (1, 8, B), 1)
    for t in range(B // 8):
        k0 = 8 * t
        p = blk[:, k0 : k0 + 8, :]
        cols = [jnp.broadcast_to(p[:, :, k0 + m : k0 + m + 1], (S, 8, B)) for m in range(8)]
        scale = jnp.zeros((S, 8, B), F32)
        for j in range(8):
            d = cols[j][:, j : j + 1, :]
            rd = jnp.broadcast_to(1.0 / d, (S, 8, B))
            scale = jnp.where(row == j, rd, scale)
            if j < 7:
                mult = jnp.where(row > j, cols[j] * rd, 0.0)
                prow = jnp.where(lane[:, :1] == k0 + j, 1.0, p[:, j : j + 1, :])
                p = jnp.where((lane == k0 + j) & (row > j), 0.0, p) - mult * prow
                for m in range(j + 1, 8):
                    cols[m] = cols[m] - mult * cols[m][:, j : j + 1, :]
        blk[:, k0 : k0 + 8, :] = p
        if t < B // 8 - 1:
            off = lane - k0
            scaled = p * scale
            aug = jnp.where((off > row) & (off < 8), 0.0, jnp.where(off == row, 1.0, p))
            inblk = (lane >= k0) & (lane < k0 + 8)
            r0 = k0 + 8
            for s in range(S):
                upd = rank8(scaled[s], aug[s])
                blk[s, r0:, :] = jnp.where(inblk[0, :1], 0.0, blk[s, r0:, :]) - upd[r0:, :]


def factor(work, blk, tri, steps, begin=0, end=None):
    S = work.shape[0]
    r_i = lax.broadcasted_iota(jnp.int32, (B, B), 0)
    c_i = lax.broadcasted_iota(jnp.int32, (B, B), 1)

    def body(j, _):
        rows = pl.ds(pl.multiple_of(j * B, B), B)
        blk[...] = work[:, rows, rows]
        eliminate_block(blk)
        for s in range(S):
            a = blk[s]
            d = jnp.sum(jnp.where(r_i == c_i, a, 0.0), axis=1, keepdims=True)
            t = jnp.where(c_i < r_i, a, jnp.where(c_i == r_i, 1.0, 0.0)) * lax.rsqrt(d)
            tri[s, j] = t
            work[s, rows, :] = dot_n(t, work[s, rows, :])

            def update(i, _, s=s):
                rows_i = pl.ds(pl.multiple_of(i * B, B), B)
                work[s, rows_i, :] -= dot_t(work[s, rows, rows_i], work[s, rows, :])
                return 0

            lax.fori_loop(j + 1, steps, update, 0)
        return 0

    lax.fori_loop(begin, steps if end is None else end, body, 0)


def scenario_kernel(kkt, border, lcol, lrow, rcol, head, y, ids, work, tri, blk):
    S, n, _ = kkt.shape
    panel = head.shape[0]
    half = y.shape[1] // S
    cols = y.shape[2]
    lanes = lax.broadcasted_iota(jnp.int32, (n, panel + half), 1)
    first_lane = lax.broadcasted_iota(jnp.int32, (n, B), 1) == 0
    for s in range(S):
        own = lcol[s]
        before = jnp.where(lrow[s : s + 1, :] < own, 1.0, 0.0)
        rank = jnp.sum(before, axis=1, keepdims=True).astype(jnp.int32)
        place = jnp.where(own < panel, own, panel + rank - (n - half))
        hot = jnp.where(lanes == place, 1.0, 0.0)
        ids[s : s + 1, :] = jnp.sum(
            jnp.where(lanes[:, panel:] == place, own, 0), axis=0, keepdims=True
        )
        work[s, :, :n] = kkt[s]
        work[s, :, n : n + panel + half] = jnp.dot(
            border[s], hot.astype(BF16), preferred_element_type=F32
        )
        work[s, :, n + panel + half :] = jnp.where(first_lane, rcol[s], 0.0)
    factor(work, blk, tri, n // B)
    total = None
    for s in range(S):
        wp = work[s, :, n : n + panel]
        wo = work[s, :, n + panel : n + panel + half]
        part = dot_t(wp, wp)
        total = part if total is None else total + part
        out = dot_t(wo, wp)
        for c in range(panel // cols):
            y[c, s * half : (s + 1) * half] = out[:, c * cols : (c + 1) * cols]
    head[...] = total


def scatter_kernel(ids, y, dense):
    dense[...] = jnp.zeros_like(dense)
    groups, half = ids.shape
    run = 32

    def body(i, _):
        s = i // (half // run)
        r0 = pl.multiple_of(lax.rem(i, half // run) * run, run)
        where = [ids[s, r0 + k] for k in range(run)]
        tile = y[pl.ds(pl.multiple_of(i * run, run), run), :]
        old = [dense[pl.ds(where[k], 1), :] for k in range(run)]
        for k in range(run):
            dense[pl.ds(where[k], 1), :] = old[k] + tile[k : k + 1, :]
        return 0

    lax.fori_loop(0, groups * half // run, body, 0)


def place_of():
    scen, crow, ccol = (lax.axis_index(a) for a in ("scen", "crow", "ccol"))
    return scen // 2, scen % 2, crow // 2, crow % 2, ccol


def device(x, z_hi, z_lo, core, y):
    return (x * 2 + z_hi, z_lo * 2 + core, y)


def greet(others):
    barrier = pltpu.get_barrier_semaphore()
    for other in others:
        pl.semaphore_signal(barrier, inc=1, device_id=other, device_id_type=MESH)
    pl.semaphore_wait(barrier, len(others))


class Copies:
    def __init__(self, send, recv):
        self.send, self.recv, self.used = send, recv, 0

    def start(self, src, dst, other):
        k = self.used
        self.used += 1
        copy = pltpu.make_async_remote_copy(
            src_ref=src,
            dst_ref=dst,
            send_sem=self.send.at[k],
            recv_sem=self.recv.at[k],
            device_id=other,
            device_id_type=MESH,
        )
        copy.start()
        return copy


HEAD_COPIES = 44


def exchange_kernel(head, y, ids, total, y_all, ids_all, got_core, acc, got_x, acc_x, got_yz, send, recv):
    x, z_hi, z_lo, core, c = place_of()
    num_cols = y.shape[0]
    n = head.shape[0]
    wide = n // 2
    rows_x = n // 4
    z = z_hi * 2 + z_lo
    g = z * num_cols + c
    group = 4 * num_cols
    sibling = device(x, z_hi, z_lo, 1 - core, c)
    x_others = [device((x + p) % 4, z_hi, z_lo, core, c) for p in range(1, 4)]
    yz_index = [(g + p) % group for p in range(1, group)]
    yz_others = [
        device(x, o // num_cols // 2, o // num_cols % 2, core, o % num_cols) for o in yz_index
    ]
    c_index = [(c + p) % num_cols for p in range(1, num_cols)]
    c_others = [device(x, z_hi, z_lo, core, o) for o in c_index]
    greet([sibling] + x_others + yz_others)
    copies = Copies(send, recv)
    own = pl.ds(pl.multiple_of(core * wide, wide), wide)
    far = pl.ds(pl.multiple_of((1 - core) * wide, wide), wide)

    pair = copies.start(head.at[:, far], got_core, sibling)
    back = []
    for o, other in zip(c_index, c_others):
        back.append(copies.start(ids, ids_all.at[c], other))
        back.append(copies.start(y.at[o], y_all.at[c], other))
    ids_all[c] = ids[...]
    y_all[c] = y[c]
    pair.wait()
    acc[...] = head[:, own] + got_core[...]
    moves = [
        copies.start(
            acc.at[pl.ds(pl.multiple_of((x + p) % 4 * rows_x, rows_x), rows_x), :],
            got_x.at[p - 1],
            x_others[p - 1],
        )
        for p in range(1, 4)
    ]
    for m in moves:
        m.wait()
    mine = pl.ds(pl.multiple_of(x * rows_x, rows_x), rows_x)
    acc_x[...] = acc[mine, :] + got_x[0] + got_x[1] + got_x[2]
    moves = [
        copies.start(
            acc_x.at[pl.ds(pl.multiple_of(o * 8, 8), 8), :], got_yz.at[p], other
        )
        for p, (o, other) in enumerate(zip(yz_index, yz_others))
    ]
    for m in moves:
        m.wait()
    tile = acc_x[pl.ds(pl.multiple_of(g * 8, 8), 8), :]
    for p in range(group - 1):
        tile = tile + got_yz[p]
    at = pl.ds(pl.multiple_of(x * rows_x + g * 8, 8), 8)
    total[at, own] = tile
    moves = [copies.start(total.at[at, own], total.at[at, own], other) for other in yz_others]
    for m in moves:
        m.wait()
    moves = [copies.start(total.at[mine, own], total.at[mine, own], other) for other in x_others]
    for m in moves:
        m.wait()
    copies.start(total.at[:, own], total.at[:, own], sibling).wait()
    for m in back:
        m.wait()


def panel_kernel(
    dense, head, diag, rhs, solved, tri_s,
    out, step, second,
    got_core, acc, got, chunk, rows, work, tri, blk, send, recv,
):
    x, z_hi, z_lo, core, c = place_of()
    num_cols = rows.shape[0]
    n = head.shape[0]
    size, cols = chunk.shape
    block = acc.shape[1]
    scen = x * 2 + z_hi
    h = scen * 2 + z_lo
    group = 2 * block // size
    sibling = device(x, z_hi, z_lo, 1 - core, c)
    h_index = [(h + p) % group for p in range(1, group)]
    h_others = [(o // 2, (o % 2) * 2 + core, c) for o in h_index]
    c_others = [device(x, z_hi, z_lo, core, (c + p) % num_cols) for p in range(1, num_cols)]
    greet([sibling] + h_others + c_others)
    copies = Copies(send, recv)

    def part(z_at, core_at):
        return pl.ds(pl.multiple_of((z_at * 2 + core_at) * block, block), block)

    pairs = [
        copies.start(dense.at[part(k, 1 - core), :], got_core.at[k], sibling) for k in range(2)
    ]
    for k in range(2):
        pairs[k].wait()
        acc[k] = dense[part(k, core), :] + got_core[k]
    moves = [
        copies.start(
            acc.at[o % 2, pl.ds(pl.multiple_of(o // 2 * size, size), size), :], got.at[p], other
        )
        for p, (o, other) in enumerate(zip(h_index, h_others))
    ]

    r_i = lax.broadcasted_iota(jnp.int32, (n, n), 0)
    c_i = lax.broadcasted_iota(jnp.int32, (n, n), 1)
    first_lane = lax.broadcasted_iota(jnp.int32, (n, B), 1) == 0
    work[0, :, :n] = head[...] + jnp.where(r_i == c_i, diag[...], 0.0)
    work[0, :, n : 2 * n] = jnp.where(r_i == c_i, 1.0, 0.0)
    work[0, :, 2 * n :] = jnp.where(first_lane, rhs[...], 0.0)
    factor(work, blk, tri, n // B, 0, n // B - 1)

    for m in moves:
        m.wait()
    total = acc[z_lo, pl.ds(pl.multiple_of(scen * size, size), size), :]
    for p in range(group - 1):
        total = total + got[p]
    chunk[...] = total
    moves = [copies.start(chunk, rows.at[c], other) for other in c_others]
    rows[c] = total
    factor(work, blk, tri, n // B, n // B - 1, n // B)
    for m in moves:
        m.wait()

    at = pl.ds(pl.multiple_of(c * cols, cols), cols)
    lower = None
    for k in range(num_cols):
        term = dot_nt(rows[k], work[0, at, n + k * cols : n + (k + 1) * cols])
        lower = term if lower is None else lower + term
    top_at = pl.ds(pl.multiple_of(scen % 2 * size, size), size)
    r_s = lax.broadcasted_iota(jnp.int32, (cols, size), 0) + c * cols
    c_s = lax.broadcasted_iota(jnp.int32, (cols, size), 1) + scen % 2 * size
    top = jnp.where(c_s >= r_s, work[0, at, top_at], 0.0).T
    is_top = (z_lo * 2 + core == 0) & (scen * size < n)
    slot = pl.ds(pl.multiple_of(scen * size, size), size)
    out[slot, :] = jnp.where(is_top, top, lower)
    moves = [
        copies.start(out.at[slot, :], out.at[slot, :], ((scen + p) % 8, z_lo * 2 + core, c))
        for p in range(1, 8)
    ]
    inner = work[0, :, 2 * n : 2 * n + 1]
    step[...] = jnp.sum(work[0, :, n : 2 * n] * inner, axis=0, keepdims=True)
    second_step(solved, tri_s, step, second)
    for m in moves:
        m.wait()


def second_step(work, tri, step, out):
    S, n, _ = work.shape
    panel = step.shape[1]
    f = step[...]
    moved = [
        work[s, :, n + panel + panel // 2 : n + panel + panel // 2 + 1]
        - jnp.sum(work[s, :, n : n + panel] * f, axis=1, keepdims=True)
        for s in range(S)
    ]
    x = [[None] * (n // B) for _ in range(S)]
    for j in reversed(range(n // B)):
        rows = slice(j * B, (j + 1) * B)
        for s in range(S):
            left = moved[s][rows]
            for i in range(j + 1, n // B):
                left = left - jnp.sum(
                    work[s, rows, i * B : (i + 1) * B] * x[s][i], axis=1, keepdims=True
                )
            x[s][j] = jnp.sum(tri[s, j] * left, axis=0, keepdims=True)
            out[s : s + 1, j * B : (j + 1) * B] = x[s][j]


VMEM = pl.BlockSpec(memory_space=pltpu.VMEM)
SMEM = pl.BlockSpec(memory_space=pltpu.SMEM)
MESH = pl.DeviceIdType.MESH
LIMIT = 60 * 2**20


def call(kernel, outs, in_specs, scratch=(), collective=None):
    remote = {} if collective is None else dict(collective_id=collective, has_side_effects=True)
    return pl.pallas_call(
        kernel,
        out_shape=outs,
        in_specs=in_specs,
        out_specs=tuple(VMEM for _ in outs) if isinstance(outs, tuple) else VMEM,
        scratch_shapes=list(scratch),
        compiler_params=pltpu.CompilerParams(vmem_limit_bytes=LIMIT, **remote),
        cost_estimate=pl.CostEstimate(flops=10**10, bytes_accessed=2**20, transcendentals=0),
    )


def shape(*dims, dtype=F32):
    return jax.ShapeDtypeStruct(dims, dtype)


def per_device(kkt, border, linked, rhs_second, rhs_first, first_diag):
    S, n, _ = kkt.shape
    panel = rhs_first.shape[0]
    num_rows = lax.axis_size("crow")
    num_cols = lax.axis_size("ccol")
    num_scen = lax.axis_size("scen")
    tile_rows = FIRST // num_rows
    cols = panel // num_cols
    half = n - INSIDE
    width = n + panel + half + B
    dma = pltpu.SemaphoreType.DMA
    head, y, ids, solved, tri = call(
        scenario_kernel,
        (
            shape(panel, panel),
            shape(num_cols, S * half, cols),
            shape(S, half, dtype=jnp.int32),
            shape(S, n, width),
            shape(S, n // B, B, B),
        ),
        [VMEM] * 5,
        [pltpu.VMEM((S, B, B), F32)],
    )(kkt, border, linked[:, :, None], linked, rhs_second[:, :, None])
    group = 4 * num_cols
    total, y_all, ids_all = call(
        exchange_kernel,
        (
            shape(panel, panel),
            shape(num_cols, S * half, cols),
            shape(num_cols, S * half // B, B, dtype=jnp.int32),
        ),
        [VMEM] * 3,
        [
            pltpu.VMEM((panel, panel // 2), F32),
            pltpu.VMEM((panel, panel // 2), F32),
            pltpu.VMEM((3, panel // 4, panel // 2), F32),
            pltpu.VMEM((panel // 4, panel // 2), F32),
            pltpu.VMEM((group - 1, 8, panel // 2), F32),
            dma((HEAD_COPIES,)),
            dma((HEAD_COPIES,)),
        ],
        collective=0,
    )(head, y, ids.reshape(S * half // B, B))
    dense = call(scatter_kernel, shape(FIRST, cols), [SMEM, VMEM])(
        ids_all.reshape(num_cols * S, half), y_all.reshape(num_cols * S * half, cols)
    )
    size = tile_rows // num_scen
    panel_factor, step, second = call(
        panel_kernel,
        (shape(tile_rows, cols), shape(1, panel), shape(S, n)),
        [VMEM] * 6,
        [
            pltpu.VMEM((2, tile_rows, cols), F32),
            pltpu.VMEM((2, tile_rows, cols), F32),
            pltpu.VMEM((2 * num_scen - 1, size, cols), F32),
            pltpu.VMEM((size, cols), F32),
            pltpu.VMEM((num_cols, size, cols), F32),
            pltpu.VMEM((1, panel, 2 * panel + B), F32),
            pltpu.VMEM((1, panel // B, B, B), F32),
            pltpu.VMEM((1, B, B), F32),
            dma((HEAD_COPIES,)),
            dma((HEAD_COPIES,)),
        ],
        collective=1,
    )(dense, total, first_diag[None, :], rhs_first[:, None], solved, tri)
    return (panel_factor, step[0], second)


def solution(mesh):
    placed = (
        P(("scen", "crow", "ccol"), None, None),
        P(("scen", "crow", "ccol"), None, None),
        P(("scen", "crow", "ccol"), None),
        P(("scen", "crow", "ccol"), None),
        P(),
        P(),
    )
    return jax.shard_map(
        per_device,
        mesh=mesh,
        in_specs=placed,
        out_specs=(P("crow", "ccol"), P(), P(("scen", "crow", "ccol"), None)),
        check_vma=False,
    )
```

```python
import jax
import jax.numpy as jnp
from jax import lax
from jax.experimental import pallas as pl
from jax.experimental.pallas import tpu as pltpu
from jax.sharding import PartitionSpec as P

F32 = jnp.float32
BF16 = jnp.bfloat16
B = 128
FIRST = 8192
INSIDE = 256


def split2(x):
    hi = x.astype(BF16)
    lo = (x - hi.astype(F32)).astype(BF16)
    return hi, lo


def dot_t(x, y):
    xh, xl = split2(x)
    yh, yl = split2(y)
    return lax.dot_general(
        jnp.concatenate([xh, xh, xl], axis=0),
        jnp.concatenate([yh, yl, yh], axis=0),
        (((0,), (0,)), ((), ())),
        preferred_element_type=F32,
    )


def dot_n(x, y):
    xh, xl = split2(x)
    yh, yl = split2(y)
    return lax.dot_general(
        jnp.concatenate([xh, xh, xl], axis=1),
        jnp.concatenate([yh, yl, yh], axis=0),
        (((1,), (0,)), ((), ())),
        preferred_element_type=F32,
    )


def dot_nt(x, y):
    xh, xl = split2(x)
    yh, yl = split2(y)
    return lax.dot_general(
        jnp.concatenate([xh, xh, xl], axis=1),
        jnp.concatenate([yh, yl, yh], axis=1),
        (((1,), (1,)), ((), ())),
        preferred_element_type=F32,
    )


def pieces3(x):
    h = x.astype(BF16).astype(F32)
    r = x - h
    m = r.astype(BF16).astype(F32)
    return h, m, r - m


def rank8(x, y):
    xh, xm, xl = pieces3(x)
    yh, ym, yl = pieces3(y)
    return lax.dot_general(
        jnp.concatenate([xh, xh, xm, xm, xh, xl], axis=0).astype(BF16),
        jnp.concatenate([yh, ym, yh, ym, yl, yh], axis=0).astype(BF16),
        (((0,), (0,)), ((), ())),
        preferred_element_type=F32,
    )


def eliminate_block(blk):
    S = blk.shape[0]
    lane = lax.broadcasted_iota(jnp.int32, (1, 8, B), 2)
    row = lax.broadcasted_iota(jnp.int32, (1, 8, B), 1)
    tiles = B // 8
    p = blk[:, 0:8, :]
    for t in range(tiles):
        k0 = 8 * t

        def spread(v, m):
            return jnp.broadcast_to(v[:, :, k0 + m : k0 + m + 1], (S, 8, B))

        ahead = t < tiles - 1
        q = blk[:, k0 + 8 : k0 + 16, :] if ahead else None
        cols = [spread(p, m) for m in range(8)]
        qcols = [spread(q, m) for m in range(8)] if ahead else None
        scale = jnp.zeros((S, 8, B), F32)
        for j in range(8):
            rd = jnp.broadcast_to(1.0 / cols[j][:, j : j + 1, :], (S, 8, B))
            scale = jnp.where(row == j, rd, scale)
            here = lane == k0 + j
            prow = jnp.where(here[:, :1], 1.0, p[:, j : j + 1, :])
            crow = [cols[m][:, j : j + 1, :] for m in range(8)]
            if j < 7:
                mult = jnp.where(row > j, cols[j], 0.0) * rd
                p = jnp.where(here & (row > j), 0.0, p) - mult * prow
                for m in range(j + 1, 8):
                    cols[m] = cols[m] - mult * crow[m]
            if ahead:
                mult = qcols[j] * rd
                q = jnp.where(here, 0.0, q) - mult * prow
                for m in range(j + 1, 8):
                    qcols[m] = qcols[m] - mult * crow[m]
        blk[:, k0 : k0 + 8, :] = p
        r0 = k0 + 16
        if r0 < B:
            off = lane - k0
            scaled = p * scale
            aug = jnp.where((off > row) & (off < 8), 0.0, jnp.where(off == row, 1.0, p))
            inblk = (off >= 0) & (off < 8)
            for s in range(S):
                upd = rank8(scaled[s], aug[s])
                blk[s, r0:, :] = jnp.where(inblk[0, :1], 0.0, blk[s, r0:, :]) - upd[r0:, :]
        p = q


def factor(work, blk, tri, steps, begin=0, end=None):
    S = work.shape[0]
    r_i = lax.broadcasted_iota(jnp.int32, (B, B), 0)
    c_i = lax.broadcasted_iota(jnp.int32, (B, B), 1)

    def body(j, _):
        rows = pl.ds(pl.multiple_of(j * B, B), B)
        blk[...] = work[:, rows, rows]
        eliminate_block(blk)
        for s in range(S):
            a = blk[s]
            d = jnp.sum(jnp.where(r_i == c_i, a, 0.0), axis=1, keepdims=True)
            t = jnp.where(c_i < r_i, a, jnp.where(c_i == r_i, 1.0, 0.0)) * lax.rsqrt(d)
            tri[s, j] = t
            work[s, rows, :] = dot_n(t, work[s, rows, :])

            def update(i, _, s=s):
                rows_i = pl.ds(pl.multiple_of(i * B, B), B)
                work[s, rows_i, :] -= dot_t(work[s, rows, rows_i], work[s, rows, :])
                return 0

            lax.fori_loop(j + 1, steps, update, 0)
        return 0

    lax.fori_loop(begin, steps if end is None else end, body, 0)


def place_of():
    scen, crow, ccol = (lax.axis_index(a) for a in ("scen", "crow", "ccol"))
    return scen // 2, scen % 2, crow // 2, crow % 2, ccol


def device(x, z, core, y):
    return (x * 2 + z // 2, z % 2 * 2 + core, y)


class Copies:
    def __init__(self, send, recv):
        self.send, self.recv, self.used = send, recv, 0

    def start(self, src, dst, other):
        k = self.used
        self.used += 1
        copy = pltpu.make_async_remote_copy(
            src_ref=src,
            dst_ref=dst,
            send_sem=self.send.at[k],
            recv_sem=self.recv.at[k],
            device_id=other,
            device_id_type=MESH,
        )
        copy.start()
        return copy


COPIES = 96


def at(start, size, step):
    return pl.ds(pl.multiple_of(start, step), size)


def second_step(work, tri, step, out):
    S, n, _ = work.shape
    panel = step.shape[1]
    f = step[...]
    moved = [
        work[s, :, n + panel + panel // 2 : n + panel + panel // 2 + 1]
        - jnp.sum(work[s, :, n : n + panel] * f, axis=1, keepdims=True)
        for s in range(S)
    ]
    x = [[None] * (n // B) for _ in range(S)]
    for j in reversed(range(n // B)):
        rows = slice(j * B, (j + 1) * B)
        for s in range(S):
            left = moved[s][rows]
            for i in range(j + 1, n // B):
                left = left - jnp.sum(
                    work[s, rows, i * B : (i + 1) * B] * x[s][i], axis=1, keepdims=True
                )
            x[s][j] = jnp.sum(tri[s, j] * left, axis=0, keepdims=True)
            out[s : s + 1, j * B : (j + 1) * B] = x[s][j]


def whole_kernel(
    kkt, border, linked, rhs_second, diag, rhs,
    out, step, second,
    work, tri_s, blk_s,
    y, y_all, ids, ids_all, y_cut,
    head, got_core, acc, got_x, acc_x, got_yz, total,
    dense, far_rows, own_rows, got, chunk, rows,
    head_work, tri, blk, send, recv,
):
    S, n, _ = kkt.shape
    x, z_hi, z_lo, core, c = place_of()
    z = z_hi * 2 + z_lo
    scen = x * 2 + z_hi
    num_cols, links, cols = y.shape
    half = links // S
    panel = num_cols * cols
    block = own_rows.shape[1]
    size = chunk.shape[0]

    sibling = device(x, z, 1 - core, c)
    x_others = [device((x + p) % 4, z, core, c) for p in range(1, 4)]
    g = z * num_cols + c
    group = 4 * num_cols
    yz_index = [(g + p) % group for p in range(1, group)]
    yz_others = [device(x, o // num_cols, core, o % num_cols) for o in yz_index]
    both_others = [
        device((x + p) % 4, (z + q) % 4, core, c) for p in range(1, 4) for q in range(1, 4)
    ]
    c_index = [(c + p) % num_cols for p in (1, 3, 2)]
    c_others = [device(x, z, core, o) for o in c_index]
    c_from = [(c + num_cols - p) % num_cols for p in (1, 3, 2)]
    h = scen * 2 + z_lo
    h_index = [(h + p) % 16 for p in range(1, 16)]
    h_others = [(o // 2, o % 2 * 2 + core, c) for o in h_index]
    barrier = pltpu.get_barrier_semaphore()
    greeted = [sibling] + x_others + yz_others + both_others
    for other in greeted:
        pl.semaphore_signal(barrier, inc=1, device_id=other, device_id_type=MESH)
    copies = Copies(send, recv)

    lanes = lax.broadcasted_iota(jnp.int32, (n, panel + half), 1)
    first_lane = lax.broadcasted_iota(jnp.int32, (n, B), 1) == 0
    links_t = jnp.concatenate([linked[...]] * (8 // S), axis=0).T
    rhs_t = jnp.concatenate([rhs_second[...]] * (8 // S), axis=0).T
    for s in range(S):
        own = links_t[:, s : s + 1]
        before = jnp.where(linked[s : s + 1, :] < own, 1.0, 0.0)
        rank = jnp.sum(before, axis=1, keepdims=True).astype(jnp.int32)
        place = jnp.where(own < panel, own, panel + rank - (n - half))
        hot = jnp.where(lanes == place, 1.0, 0.0)
        row_ids = jnp.sum(jnp.where(lanes[:, panel:] == place, own, 0), axis=0, keepdims=True)
        for q in range(half // B):
            k = s * (half // B) + q
            ids[k : k + 1, :] = row_ids[:, q * B : (q + 1) * B]
        work[s, :, :n] = kkt[s]
        work[s, :, n : n + panel + half] = jnp.dot(
            border[s], hot.astype(BF16), preferred_element_type=F32
        )
        work[s, :, n + panel + half :] = jnp.where(first_lane, rhs_t[:, s : s + 1], 0.0)
    factor(work, blk_s, tri_s, n // B)

    pl.semaphore_wait(barrier, len(greeted))
    from_c = [[copies.start(ids, ids_all.at[c], other)] for other in c_others]
    for s in range(S):
        wp = work[s, :, n : n + panel]
        wo = work[s, :, n + panel : n + panel + half]
        pair = dot_t(wo, wp)
        for o in range(num_cols):
            y[o, s * half : (s + 1) * half] = pair[:, o * cols : (o + 1) * cols]
        span = pl.ds(s * half, half)
        for k, (o, other) in enumerate(zip(c_index, c_others)):
            from_c[k].append(copies.start(y.at[o, span], y_all.at[c, span], other))
    ids_all[c] = ids[...]
    y_all[c] = y[c]
    for s in range(S):
        wp = work[s, :, n : n + panel]
        part = dot_t(wp, wp)
        head[...] = part if s == 0 else head[...] + part

    run = 512
    base = lax.broadcasted_iota(jnp.int32, (run, B), 0)

    def place_rows(source, blocks, first):
        for k in range(2):
            b = k * 2 + blocks

            def body(i, _, b=b):
                r0 = b * block + i * run
                where = [
                    jnp.where(base + r0 == ids_all[source, q : q + 1, :], 1.0, 0.0).astype(BF16)
                    for q in range(links // B)
                ]
                put = jnp.dot(
                    jnp.concatenate(where, axis=1), y_cut[...], preferred_element_type=F32
                )
                put = put[:, :cols] + put[:, cols:]
                to = at(r0, run, run)
                dense[to, :] = put if first else dense[to, :] + put
                return 0

            lax.fori_loop(0, block // run, body, 0)

    def cut(source):
        hi, lo = split2(y_all[source])
        y_cut[:, :cols] = hi
        y_cut[:, cols:] = lo

    wide = n // 2
    own_l = at(core * wide, wide, wide)
    far_l = at((1 - core) * wide, wide, wide)
    pair = copies.start(head.at[:, far_l], got_core, sibling)
    cut(c)
    place_rows(c, 1 - core, True)
    pair.wait()
    acc[...] = head[:, own_l] + got_core[...]
    rows_x = n // 4
    moves = [
        copies.start(acc.at[at((x + p) % 4 * rows_x, rows_x, rows_x), :], got_x.at[p - 1], other)
        for p, other in zip(range(1, 4), x_others)
    ]
    place_rows(c, core, True)
    for m in moves:
        m.wait()
    mine = at(x * rows_x, rows_x, rows_x)
    acc_x[...] = acc[mine, :] + got_x[0] + got_x[1] + got_x[2]
    moves = [
        copies.start(acc_x.at[at(o * 8, 8, 8), :], got_yz.at[p], other)
        for p, (o, other) in enumerate(zip(yz_index, yz_others))
    ]
    for m in from_c[0]:
        m.wait()
    cut(c_from[0])
    place_rows(c_from[0], 1 - core, False)
    for m in moves:
        m.wait()
    tile = acc_x[at(g * 8, 8, 8), :]
    for p in range(group - 1):
        tile = tile + got_yz[p]
    spot = at(x * rows_x + g * 8, 8, 8)
    total[spot, own_l] = tile
    moves = [copies.start(total.at[spot, own_l], total.at[spot, own_l], o) for o in yz_others]
    place_rows(c_from[0], core, False)
    for m in moves:
        m.wait()
    moves = [copies.start(total.at[mine, own_l], total.at[mine, own_l], o) for o in x_others]
    for m in from_c[1]:
        m.wait()
    cut(c_from[1])
    place_rows(c_from[1], 1 - core, False)
    for m in moves:
        m.wait()
    pair = copies.start(total.at[:, own_l], total.at[:, own_l], sibling)
    place_rows(c_from[1], core, False)
    for m in from_c[2]:
        m.wait()
    cut(c_from[2])
    place_rows(c_from[2], 1 - core, False)

    fars = [
        copies.start(dense.at[at((k * 2 + 1 - core) * block, block, block), :], far_rows.at[k], sibling)
        for k in range(2)
    ]
    place_rows(c_from[2], core, False)
    pair.wait()
    for k in range(2):
        fars[k].wait()
        own_rows[k] = dense[at((k * 2 + core) * block, block, block), :] + far_rows[k]
    moves = [
        copies.start(own_rows.at[o % 2, at(o // 2 * size, size, size), :], got.at[p], other)
        for p, (o, other) in enumerate(zip(h_index, h_others))
    ]

    r_i = lax.broadcasted_iota(jnp.int32, (n, n), 0)
    c_i = lax.broadcasted_iota(jnp.int32, (n, n), 1)
    head_work[0, :, :n] = total[...] + jnp.where(r_i == c_i, diag[...], 0.0)
    head_work[0, :, n : 2 * n] = jnp.where(r_i == c_i, 1.0, 0.0)
    rhs_c = jnp.concatenate([rhs[...]] * 8, axis=0).T
    head_work[0, :, 2 * n :] = jnp.where(first_lane, rhs_c[:, :1], 0.0)
    factor(head_work, blk, tri, n // B, 0, n // B - 1)

    for m in moves:
        m.wait()
    summed = own_rows[z_lo, at(scen * size, size, size), :]
    for p in range(15):
        summed = summed + got[p]
    chunk[...] = summed
    moves = [copies.start(chunk, rows.at[c], other) for other in c_others]
    rows[c] = summed
    factor(head_work, blk, tri, n // B, n // B - 1, n // B)
    for m in moves:
        m.wait()

    own_c = at(c * cols, cols, cols)
    lower = None
    for k in range(num_cols):
        term = dot_nt(rows[k], head_work[0, own_c, n + k * cols : n + (k + 1) * cols])
        lower = term if lower is None else lower + term
    top_at = at(scen % 2 * size, size, size)
    r_s = lax.broadcasted_iota(jnp.int32, (cols, size), 0) + c * cols
    c_s = lax.broadcasted_iota(jnp.int32, (cols, size), 1) + scen % 2 * size
    top = jnp.where(c_s >= r_s, head_work[0, own_c, top_at], 0.0).T
    is_top = (z_lo * 2 + core == 0) & (scen * size < n)
    slot = at(scen * size, size, size)
    out[slot, :] = jnp.where(is_top, top, lower)
    moves = [
        copies.start(out.at[slot, :], out.at[slot, :], ((scen + p) % 8, z_lo * 2 + core, c))
        for p in range(1, 8)
    ]
    inner = head_work[0, :, 2 * n : 2 * n + 1]
    step[...] = jnp.sum(head_work[0, :, n : 2 * n] * inner, axis=0, keepdims=True)
    second_step(work, tri_s, step, second)
    for m in moves:
        m.wait()


VMEM = pl.BlockSpec(memory_space=pltpu.VMEM)
MESH = pl.DeviceIdType.MESH
LIMIT = 62 * 2**20


def shape(*dims, dtype=F32):
    return jax.ShapeDtypeStruct(dims, dtype)


def per_device(kkt, border, linked, rhs_second, rhs_first, first_diag):
    S, n, _ = kkt.shape
    panel = rhs_first.shape[0]
    num_rows = lax.axis_size("crow")
    num_cols = lax.axis_size("ccol")
    num_scen = lax.axis_size("scen")
    tile_rows = FIRST // num_rows
    cols = panel // num_cols
    half = n - INSIDE
    width = n + panel + half + B
    group = 4 * num_cols
    size = tile_rows // num_scen
    dma = pltpu.SemaphoreType.DMA
    vmem = pltpu.VMEM
    panel_factor, step, second = pl.pallas_call(
        whole_kernel,
        out_shape=(shape(tile_rows, cols), shape(1, panel), shape(S, n)),
        in_specs=[VMEM] * 6,
        out_specs=(VMEM,) * 3,
        scratch_shapes=[
            vmem((S, n, width), F32),
            vmem((S, n // B, B, B), F32),
            vmem((S, B, B), F32),
            vmem((num_cols, S * half, cols), F32),
            vmem((num_cols, S * half, cols), F32),
            vmem((S * half // B, B), jnp.int32),
            vmem((num_cols, S * half // B, B), jnp.int32),
            vmem((S * half, 2 * cols), BF16),
            vmem((panel, panel), F32),
            vmem((panel, panel // 2), F32),
            vmem((panel, panel // 2), F32),
            vmem((3, panel // 4, panel // 2), F32),
            vmem((panel // 4, panel // 2), F32),
            vmem((group - 1, 8, panel // 2), F32),
            vmem((panel, panel), F32),
            vmem((FIRST, cols), F32),
            vmem((2, tile_rows, cols), F32),
            vmem((2, tile_rows, cols), F32),
            vmem((2 * num_scen - 1, size, cols), F32),
            vmem((size, cols), F32),
            vmem((num_cols, size, cols), F32),
            vmem((1, panel, 2 * panel + B), F32),
            vmem((1, panel // B, B, B), F32),
            vmem((1, B, B), F32),
            dma((COPIES,)),
            dma((COPIES,)),
        ],
        compiler_params=pltpu.CompilerParams(
            vmem_limit_bytes=LIMIT, collective_id=0, has_side_effects=True
        ),
        cost_estimate=pl.CostEstimate(flops=10**11, bytes_accessed=2**23, transcendentals=0),
    )(kkt, border, linked, rhs_second, first_diag[None, :], rhs_first[None, :])
    return (panel_factor, step[0], second)


def solution(mesh):
    placed = (
        P(("scen", "crow", "ccol"), None, None),
        P(("scen", "crow", "ccol"), None, None),
        P(("scen", "crow", "ccol"), None),
        P(("scen", "crow", "ccol"), None),
        P(),
        P(),
    )
    return jax.shard_map(
        per_device,
        mesh=mesh,
        in_specs=placed,
        out_specs=(P("crow", "ccol"), P(), P(("scen", "crow", "ccol"), None)),
        check_vma=False,
    )
```

```python
import jax
import jax.numpy as jnp
from jax import lax
from jax.experimental import pallas as pl
from jax.experimental.pallas import tpu as pltpu
from jax.sharding import PartitionSpec as P

F32 = jnp.float32
BF16 = jnp.bfloat16
B = 128
FIRST = 8192
INSIDE = 256


def split2(x):
    hi = x.astype(BF16)
    lo = (x - hi.astype(F32)).astype(BF16)
    return hi, lo


def dot_t(x, y):
    xh, xl = split2(x)
    yh, yl = split2(y)
    return lax.dot_general(
        jnp.concatenate([xh, xh, xl], axis=0),
        jnp.concatenate([yh, yl, yh], axis=0),
        (((0,), (0,)), ((), ())),
        preferred_element_type=F32,
    )


def dot_n(x, y):
    xh, xl = split2(x)
    yh, yl = split2(y)
    return lax.dot_general(
        jnp.concatenate([xh, xh, xl], axis=1),
        jnp.concatenate([yh, yl, yh], axis=0),
        (((1,), (0,)), ((), ())),
        preferred_element_type=F32,
    )


def dot_nt(x, y):
    xh, xl = split2(x)
    yh, yl = split2(y)
    return lax.dot_general(
        jnp.concatenate([xh, xh, xl], axis=1),
        jnp.concatenate([yh, yl, yh], axis=1),
        (((1,), (1,)), ((), ())),
        preferred_element_type=F32,
    )


def pieces3(x):
    h = x.astype(BF16).astype(F32)
    r = x - h
    m = r.astype(BF16).astype(F32)
    return h, m, r - m


def rank8(x, y):
    xh, xm, xl = pieces3(x)
    yh, ym, yl = pieces3(y)
    return lax.dot_general(
        jnp.concatenate([xh, xh, xm, xm, xh, xl], axis=0).astype(BF16),
        jnp.concatenate([yh, ym, yh, ym, yl, yh], axis=0).astype(BF16),
        (((0,), (0,)), ((), ())),
        preferred_element_type=F32,
    )


def eliminate_block(blk):
    S = blk.shape[0]
    lane = lax.broadcasted_iota(jnp.int32, (1, 8, B), 2)
    row = lax.broadcasted_iota(jnp.int32, (1, 8, B), 1)
    tiles = B // 8
    p = blk[:, 0:8, :]
    for t in range(tiles):
        k0 = 8 * t

        def spread(v, m):
            return jnp.broadcast_to(v[:, :, k0 + m : k0 + m + 1], (S, 8, B))

        ahead = t < tiles - 1
        q = blk[:, k0 + 8 : k0 + 16, :] if ahead else None
        cols = [spread(p, m) for m in range(8)]
        qcols = [spread(q, m) for m in range(8)] if ahead else None
        scale = jnp.zeros((S, 8, B), F32)
        for j in range(8):
            rd = jnp.broadcast_to(1.0 / cols[j][:, j : j + 1, :], (S, 8, B))
            scale = jnp.where(row == j, rd, scale)
            here = lane == k0 + j
            prow = jnp.where(here[:, :1], 1.0, p[:, j : j + 1, :])
            crow = [cols[m][:, j : j + 1, :] for m in range(8)]
            if j < 7:
                mult = jnp.where(row > j, cols[j], 0.0) * rd
                p = jnp.where(here & (row > j), 0.0, p) - mult * prow
                for m in range(j + 1, 8):
                    cols[m] = cols[m] - mult * crow[m]
            if ahead:
                mult = qcols[j] * rd
                q = jnp.where(here, 0.0, q) - mult * prow
                for m in range(j + 1, 8):
                    qcols[m] = qcols[m] - mult * crow[m]
        blk[:, k0 : k0 + 8, :] = p
        r0 = k0 + 16
        if r0 < B:
            off = lane - k0
            scaled = p * scale
            aug = jnp.where((off > row) & (off < 8), 0.0, jnp.where(off == row, 1.0, p))
            inblk = (off >= 0) & (off < 8)
            for s in range(S):
                upd = rank8(scaled[s], aug[s])
                blk[s, r0:, :] = jnp.where(inblk[0, :1], 0.0, blk[s, r0:, :]) - upd[r0:, :]
        p = q


def factor(work, blk, tri, steps, begin=0, end=None):
    S = work.shape[0]
    r_i = lax.broadcasted_iota(jnp.int32, (B, B), 0)
    c_i = lax.broadcasted_iota(jnp.int32, (B, B), 1)

    def body(j, _):
        rows = pl.ds(pl.multiple_of(j * B, B), B)
        blk[...] = work[:, rows, rows]
        eliminate_block(blk)
        for s in range(S):
            a = blk[s]
            d = jnp.sum(jnp.where(r_i == c_i, a, 0.0), axis=1, keepdims=True)
            t = jnp.where(c_i < r_i, a, jnp.where(c_i == r_i, 1.0, 0.0)) * lax.rsqrt(d)
            tri[s, j] = t
            work[s, rows, :] = dot_n(t, work[s, rows, :])

            def update(i, _, s=s):
                rows_i = pl.ds(pl.multiple_of(i * B, B), B)
                work[s, rows_i, :] -= dot_t(work[s, rows, rows_i], work[s, rows, :])
                return 0

            lax.fori_loop(j + 1, steps, update, 0)
        return 0

    lax.fori_loop(begin, steps if end is None else end, body, 0)


def place_of():
    scen, crow, ccol = (lax.axis_index(a) for a in ("scen", "crow", "ccol"))
    return scen // 2, scen % 2, crow // 2, crow % 2, ccol


def device(x, z, core, y):
    return (x * 2 + z // 2, z % 2 * 2 + core, y)


class Copies:
    def __init__(self, send, recv):
        self.send, self.recv, self.used = send, recv, 0

    def start(self, src, dst, other):
        k = self.used
        self.used += 1
        copy = pltpu.make_async_remote_copy(
            src_ref=src,
            dst_ref=dst,
            send_sem=self.send.at[k],
            recv_sem=self.recv.at[k],
            device_id=other,
            device_id_type=MESH,
        )
        copy.start()
        return copy


COPIES = 96


def at(start, size, step):
    return pl.ds(pl.multiple_of(start, step), size)


def second_step(work, tri, step, out):
    S, n, _ = work.shape
    panel = step.shape[1]
    f = step[...]
    moved = [
        work[s, :, n + panel + panel // 2 : n + panel + panel // 2 + 1]
        - jnp.sum(work[s, :, n : n + panel] * f, axis=1, keepdims=True)
        for s in range(S)
    ]
    x = [[None] * (n // B) for _ in range(S)]
    for j in reversed(range(n // B)):
        rows = slice(j * B, (j + 1) * B)
        for s in range(S):
            left = moved[s][rows]
            for i in range(j + 1, n // B):
                left = left - jnp.sum(
                    work[s, rows, i * B : (i + 1) * B] * x[s][i], axis=1, keepdims=True
                )
            x[s][j] = jnp.sum(tri[s, j] * left, axis=0, keepdims=True)
            out[s : s + 1, j * B : (j + 1) * B] = x[s][j]


def whole_kernel(
    kkt, border, linked, rhs_second, diag, rhs,
    out, step, second,
    work, tri_s, blk_s,
    y, y_all, ids, ids_all, y_cut,
    head, got_core, acc, got_x, acc_x, got_yz, total,
    dense, far_rows, x_first, z_first, got_a, got_b, half_a, half_b, got_c, got_d, chunk, rows,
    head_work, tri, blk, send, recv,
):
    S, n, _ = kkt.shape
    x, z_hi, z_lo, core, c = place_of()
    z = z_hi * 2 + z_lo
    scen = x * 2 + z_hi
    num_cols, links, cols = y.shape
    half = links // S
    panel = num_cols * cols
    block = far_rows.shape[1]
    size = chunk.shape[0]

    sibling = device(x, z, 1 - core, c)
    x_others = [device((x + p) % 4, z, core, c) for p in range(1, 4)]
    g = z * num_cols + c
    group = 4 * num_cols
    yz_index = [(g + p) % group for p in range(1, group)]
    yz_others = [device(x, o // num_cols, core, o % num_cols) for o in yz_index]
    z_others = [device(x, (z + p) % 4, core, c) for p in range(1, 4)]
    both_others = [device((x + p) % 4, (z + 2) % 4, core, c) for p in range(1, 4)]
    c_index = [(c + p) % num_cols for p in (1, 3, 2)]
    c_others = [device(x, z, core, o) for o in c_index]
    c_from = [(c + num_cols - p) % num_cols for p in (1, 3, 2)]
    barrier = pltpu.get_barrier_semaphore()
    greeted = [sibling] + x_others + yz_others + both_others
    for other in greeted:
        pl.semaphore_signal(barrier, inc=1, device_id=other, device_id_type=MESH)
    copies = Copies(send, recv)

    lanes = lax.broadcasted_iota(jnp.int32, (n, panel + half), 1)
    first_lane = lax.broadcasted_iota(jnp.int32, (n, B), 1) == 0
    links_t = jnp.concatenate([linked[...]] * (8 // S), axis=0).T
    rhs_t = jnp.concatenate([rhs_second[...]] * (8 // S), axis=0).T
    for s in range(S):
        own = links_t[:, s : s + 1]
        before = jnp.where(linked[s : s + 1, :] < own, 1.0, 0.0)
        rank = jnp.sum(before, axis=1, keepdims=True).astype(jnp.int32)
        place = jnp.where(own < panel, own, panel + rank - (n - half))
        hot = jnp.where(lanes == place, 1.0, 0.0)
        row_ids = jnp.sum(jnp.where(lanes[:, panel:] == place, own, 0), axis=0, keepdims=True)
        for q in range(half // B):
            k = s * (half // B) + q
            ids[k : k + 1, :] = row_ids[:, q * B : (q + 1) * B]
        work[s, :, :n] = kkt[s]
        work[s, :, n : n + panel + half] = jnp.dot(
            border[s], hot.astype(BF16), preferred_element_type=F32
        )
        work[s, :, n + panel + half :] = jnp.where(first_lane, rhs_t[:, s : s + 1], 0.0)
    factor(work, blk_s, tri_s, n // B)

    pl.semaphore_wait(barrier, len(greeted))
    from_c = [[copies.start(ids, ids_all.at[c], other)] for other in c_others]
    for s in range(S):
        wp = work[s, :, n : n + panel]
        wo = work[s, :, n + panel : n + panel + half]
        pair = dot_t(wo, wp)
        for o in range(num_cols):
            y[o, s * half : (s + 1) * half] = pair[:, o * cols : (o + 1) * cols]
        span = pl.ds(s * half, half)
        for k in range(2):
            from_c[k].append(
                copies.start(y.at[c_index[k], span], y_all.at[c, span], c_others[k])
            )
    for s in range(S):
        wp = work[s, :, n : n + panel]
        part = dot_t(wp, wp)
        head[...] = part if s == 0 else head[...] + part

    run = 512
    base = lax.broadcasted_iota(jnp.int32, (run, B), 0)

    def place_rows(source, blocks, first):
        for k in range(2):
            b = k * 2 + blocks

            def body(i, _, b=b):
                r0 = b * block + i * run
                where = [
                    jnp.where(base + r0 == ids_all[source, q : q + 1, :], 1.0, 0.0).astype(BF16)
                    for q in range(links // B)
                ]
                put = jnp.dot(
                    jnp.concatenate(where, axis=1), y_cut[...], preferred_element_type=F32
                )
                put = put[:, :cols] + put[:, cols:]
                to = at(r0, run, run)
                dense[to, :] = put if first else dense[to, :] + put
                return 0

            lax.fori_loop(0, block // run, body, 0)

    def cut(source):
        hi, lo = split2(y_all[source])
        y_cut[:, :cols] = hi
        y_cut[:, cols:] = lo

    def place(k):
        for m in from_c[k]:
            m.wait()
        cut(c_from[k])
        place_rows(c_from[k], 1 - core, False)

    wide = n // 2
    own_l = at(core * wide, wide, wide)
    far_l = at((1 - core) * wide, wide, wide)
    pair = copies.start(head.at[:, far_l], got_core, sibling)
    from_c[2].append(copies.start(y.at[c_index[2]], y_all.at[c], c_others[2]))
    ids_all[c] = ids[...]
    y_all[c] = y[c]
    cut(c)
    place_rows(c, 1 - core, True)
    pair.wait()
    acc[...] = head[:, own_l] + got_core[...]
    rows_x = n // 4
    moves = [
        copies.start(acc.at[at((x + p) % 4 * rows_x, rows_x, rows_x), :], got_x.at[p - 1], other)
        for p, other in zip(range(1, 4), x_others)
    ]
    place_rows(c, core, True)
    place(0)
    place_rows(c_from[0], core, False)
    for m in moves:
        m.wait()
    mine = at(x * rows_x, rows_x, rows_x)
    acc_x[...] = acc[mine, :] + got_x[0] + got_x[1] + got_x[2]
    moves = [
        copies.start(acc_x.at[at(o * 8, 8, 8), :], got_yz.at[p], other)
        for p, (o, other) in enumerate(zip(yz_index, yz_others))
    ]
    place(1)
    place_rows(c_from[1], core, False)
    for m in moves:
        m.wait()
    tile = acc_x[at(g * 8, 8, 8), :]
    for p in range(group - 1):
        tile = tile + got_yz[p]
    spot = at(x * rows_x + g * 8, 8, 8)
    total[spot, own_l] = tile
    moves = [copies.start(total.at[spot, own_l], total.at[spot, own_l], o) for o in yz_others]
    place(2)
    fars = [
        copies.start(dense.at[at((k * 2 + 1 - core) * block, block, block), :], far_rows.at[k], sibling)
        for k in range(2)
    ]
    place_rows(c_from[2], core, False)
    for m in moves:
        m.wait()
    moves = [copies.start(total.at[mine, own_l], total.at[mine, own_l], o) for o in x_others]

    piece = size // 2
    for k in range(2):
        fars[k].wait()
        for d in range(8):
            to_x, to_z = d // 2, d % 2 * 2 + k
            r0 = d * size
            from_own = (k * 2 + core) * block + r0
            x_first[to_x, to_z] = dense[at(from_own, piece, piece), :] + far_rows[k, r0 : r0 + piece]
            r0 += piece
            z_first[to_z, to_x] = (
                dense[at(from_own + piece, piece, piece), :] + far_rows[k, r0 : r0 + piece]
            )
    steps = []
    for p in range(1, 4):
        steps.append(copies.start(x_first.at[(x + p) % 4], got_a.at[p - 1], x_others[p - 1]))
        steps.append(copies.start(z_first.at[(z + p) % 4], got_b.at[p - 1], z_others[p - 1]))
    for m in moves:
        m.wait()
    pair = copies.start(total.at[:, own_l], total.at[:, own_l], sibling)
    pair.wait()

    r_i = lax.broadcasted_iota(jnp.int32, (n, n), 0)
    c_i = lax.broadcasted_iota(jnp.int32, (n, n), 1)
    head_work[0, :, :n] = total[...] + jnp.where(r_i == c_i, diag[...], 0.0)
    head_work[0, :, n : 2 * n] = jnp.where(r_i == c_i, 1.0, 0.0)
    rhs_c = jnp.concatenate([rhs[...]] * 8, axis=0).T
    head_work[0, :, 2 * n :] = jnp.where(first_lane, rhs_c[:, :1], 0.0)
    factor(head_work, blk, tri, n // B, 0, n // B - 2)

    for m in steps:
        m.wait()
    half_a[...] = x_first[x] + got_a[0] + got_a[1] + got_a[2]
    half_b[...] = z_first[z] + got_b[0] + got_b[1] + got_b[2]
    steps = []
    for p in range(1, 4):
        steps.append(copies.start(half_a.at[(z + p) % 4], got_c.at[p - 1], z_others[p - 1]))
        steps.append(copies.start(half_b.at[(x + p) % 4], got_d.at[p - 1], x_others[p - 1]))
    factor(head_work, blk, tri, n // B, n // B - 2, n // B - 1)
    for m in steps:
        m.wait()
    chunk[:piece] = half_a[z] + got_c[0] + got_c[1] + got_c[2]
    chunk[piece:] = half_b[x] + got_d[0] + got_d[1] + got_d[2]
    moves = [copies.start(chunk, rows.at[c], other) for other in c_others]
    rows[c] = chunk[...]
    factor(head_work, blk, tri, n // B, n // B - 1, n // B)
    for m in moves:
        m.wait()

    own_c = at(c * cols, cols, cols)
    lower = None
    for k in range(num_cols):
        term = dot_nt(rows[k], head_work[0, own_c, n + k * cols : n + (k + 1) * cols])
        lower = term if lower is None else lower + term
    top_at = at(scen % 2 * size, size, size)
    r_s = lax.broadcasted_iota(jnp.int32, (cols, size), 0) + c * cols
    c_s = lax.broadcasted_iota(jnp.int32, (cols, size), 1) + scen % 2 * size
    top = jnp.where(c_s >= r_s, head_work[0, own_c, top_at], 0.0).T
    is_top = (z_lo * 2 + core == 0) & (scen * size < n)
    slot = at(scen * size, size, size)
    out[slot, :] = jnp.where(is_top, top, lower)
    moves = [
        copies.start(out.at[slot, :], out.at[slot, :], ((scen + p) % 8, z_lo * 2 + core, c))
        for p in range(1, 8)
    ]
    inner = head_work[0, :, 2 * n : 2 * n + 1]
    step[...] = jnp.sum(head_work[0, :, n : 2 * n] * inner, axis=0, keepdims=True)
    second_step(work, tri_s, step, second)
    for m in moves:
        m.wait()


VMEM = pl.BlockSpec(memory_space=pltpu.VMEM)
MESH = pl.DeviceIdType.MESH
LIMIT = 62 * 2**20


def shape(*dims, dtype=F32):
    return jax.ShapeDtypeStruct(dims, dtype)


def per_device(kkt, border, linked, rhs_second, rhs_first, first_diag):
    S, n, _ = kkt.shape
    panel = rhs_first.shape[0]
    num_rows = lax.axis_size("crow")
    num_cols = lax.axis_size("ccol")
    num_scen = lax.axis_size("scen")
    tile_rows = FIRST // num_rows
    cols = panel // num_cols
    half = n - INSIDE
    width = n + panel + half + B
    group = 4 * num_cols
    size = tile_rows // num_scen
    dma = pltpu.SemaphoreType.DMA
    vmem = pltpu.VMEM
    panel_factor, step, second = pl.pallas_call(
        whole_kernel,
        out_shape=(shape(tile_rows, cols), shape(1, panel), shape(S, n)),
        in_specs=[VMEM] * 6,
        out_specs=(VMEM,) * 3,
        scratch_shapes=[
            vmem((S, n, width), F32),
            vmem((S, n // B, B, B), F32),
            vmem((S, B, B), F32),
            vmem((num_cols, S * half, cols), F32),
            vmem((num_cols, S * half, cols), F32),
            vmem((S * half // B, B), jnp.int32),
            vmem((num_cols, S * half // B, B), jnp.int32),
            vmem((S * half, 2 * cols), BF16),
            vmem((panel, panel), F32),
            vmem((panel, panel // 2), F32),
            vmem((panel, panel // 2), F32),
            vmem((3, panel // 4, panel // 2), F32),
            vmem((panel // 4, panel // 2), F32),
            vmem((group - 1, 8, panel // 2), F32),
            vmem((panel, panel), F32),
            vmem((FIRST, cols), F32),
            vmem((2, tile_rows, cols), F32),
            vmem((4, 4, size // 2, cols), F32),
            vmem((4, 4, size // 2, cols), F32),
            vmem((3, 4, size // 2, cols), F32),
            vmem((3, 4, size // 2, cols), F32),
            vmem((4, size // 2, cols), F32),
            vmem((4, size // 2, cols), F32),
            vmem((3, size // 2, cols), F32),
            vmem((3, size // 2, cols), F32),
            vmem((size, cols), F32),
            vmem((num_cols, size, cols), F32),
            vmem((1, panel, 2 * panel + B), F32),
            vmem((1, panel // B, B, B), F32),
            vmem((1, B, B), F32),
            dma((COPIES,)),
            dma((COPIES,)),
        ],
        compiler_params=pltpu.CompilerParams(
            vmem_limit_bytes=LIMIT, collective_id=0, has_side_effects=True
        ),
        cost_estimate=pl.CostEstimate(flops=10**11, bytes_accessed=2**23, transcendentals=0),
    )(kkt, border, linked, rhs_second, first_diag[None, :], rhs_first[None, :])
    return (panel_factor, step[0], second)


def solution(mesh):
    placed = (
        P(("scen", "crow", "ccol"), None, None),
        P(("scen", "crow", "ccol"), None, None),
        P(("scen", "crow", "ccol"), None),
        P(("scen", "crow", "ccol"), None),
        P(),
        P(),
    )
    return jax.shard_map(
        per_device,
        mesh=mesh,
        in_specs=placed,
        out_specs=(P("crow", "ccol"), P(), P(("scen", "crow", "ccol"), None)),
        check_vma=False,
    )
```

```python
import jax
import jax.numpy as jnp
from jax import lax
from jax.experimental import pallas as pl
from jax.experimental.pallas import tpu as pltpu
from jax.sharding import PartitionSpec as P

F32 = jnp.float32
BF16 = jnp.bfloat16
B = 128
FIRST = 8192
INSIDE = 256


def split2(x):
    hi = x.astype(BF16)
    lo = (x - hi.astype(F32)).astype(BF16)
    return hi, lo


def dot_t(x, y):
    xh, xl = split2(x)
    yh, yl = split2(y)
    return lax.dot_general(
        jnp.concatenate([xh, xh, xl], axis=0),
        jnp.concatenate([yh, yl, yh], axis=0),
        (((0,), (0,)), ((), ())),
        preferred_element_type=F32,
    )


def dot_n(x, y):
    xh, xl = split2(x)
    yh, yl = split2(y)
    return lax.dot_general(
        jnp.concatenate([xh, xh, xl], axis=1),
        jnp.concatenate([yh, yl, yh], axis=0),
        (((1,), (0,)), ((), ())),
        preferred_element_type=F32,
    )


def dot_nt(x, y):
    xh, xl = split2(x)
    yh, yl = split2(y)
    return lax.dot_general(
        jnp.concatenate([xh, xh, xl], axis=1),
        jnp.concatenate([yh, yl, yh], axis=1),
        (((1,), (1,)), ((), ())),
        preferred_element_type=F32,
    )


def pieces3(x):
    h = x.astype(BF16).astype(F32)
    r = x - h
    m = r.astype(BF16).astype(F32)
    return h, m, r - m


def rank8(x, y):
    xh, xm, xl = pieces3(x)
    yh, ym, yl = pieces3(y)
    return lax.dot_general(
        jnp.concatenate([xh, xh, xm, xm, xh, xl], axis=0).astype(BF16),
        jnp.concatenate([yh, ym, yh, ym, yl, yh], axis=0).astype(BF16),
        (((0,), (0,)), ((), ())),
        preferred_element_type=F32,
    )


def eliminate_block(blk):
    S = blk.shape[0]
    lane = lax.broadcasted_iota(jnp.int32, (1, 8, B), 2)
    row = lax.broadcasted_iota(jnp.int32, (1, 8, B), 1)
    tiles = B // 8
    p = blk[:, 0:8, :]
    for t in range(tiles):
        k0 = 8 * t

        def spread(v, m):
            return jnp.broadcast_to(v[:, :, k0 + m : k0 + m + 1], (S, 8, B))

        ahead = t < tiles - 1
        q = blk[:, k0 + 8 : k0 + 16, :] if ahead else None
        cols = [spread(p, m) for m in range(8)]
        qcols = [spread(q, m) for m in range(8)] if ahead else None
        scale = jnp.zeros((S, 8, B), F32)
        for j in range(8):
            rd = jnp.broadcast_to(1.0 / cols[j][:, j : j + 1, :], (S, 8, B))
            scale = jnp.where(row == j, rd, scale)
            here = lane == k0 + j
            prow = jnp.where(here[:, :1], 1.0, p[:, j : j + 1, :])
            crow = [cols[m][:, j : j + 1, :] for m in range(8)]
            if j < 7:
                mult = jnp.where(row > j, cols[j], 0.0) * rd
                p = jnp.where(here & (row > j), 0.0, p) - mult * prow
                for m in range(j + 1, 8):
                    cols[m] = cols[m] - mult * crow[m]
            if ahead:
                mult = qcols[j] * rd
                q = jnp.where(here, 0.0, q) - mult * prow
                for m in range(j + 1, 8):
                    qcols[m] = qcols[m] - mult * crow[m]
        blk[:, k0 : k0 + 8, :] = p
        r0 = k0 + 16
        if r0 < B:
            off = lane - k0
            scaled = p * scale
            aug = jnp.where((off > row) & (off < 8), 0.0, jnp.where(off == row, 1.0, p))
            inblk = (off >= 0) & (off < 8)
            for s in range(S):
                upd = rank8(scaled[s], aug[s])
                blk[s, r0:, :] = jnp.where(inblk[0, :1], 0.0, blk[s, r0:, :]) - upd[r0:, :]
        p = q


def factor(work, blk, tri, begin, end, unit):
    S, n, width = work.shape
    steps = n // B
    r_i = lax.broadcasted_iota(jnp.int32, (B, B), 0)
    c_i = lax.broadcasted_iota(jnp.int32, (B, B), 1)

    def body(j, _):
        rows = pl.ds(pl.multiple_of(j * B, B), B)
        blk[...] = work[:, rows, rows]
        eliminate_block(blk)
        for jj in range(begin, end):

            @pl.when(j == jj)
            def _(jj=jj):
                r0 = jj * B
                r1 = r0 + B
                stop = n + r1 if unit else width
                for s in range(S):
                    a = blk[s]
                    d = jnp.sum(jnp.where(r_i == c_i, a, 0.0), axis=1, keepdims=True)
                    t = jnp.where(c_i < r_i, a, jnp.where(c_i == r_i, 1.0, 0.0)) * lax.rsqrt(d)
                    tri[s, jj] = t
                    v = dot_n(t, work[s, r0:r1, r0:stop])
                    work[s, r0:r1, r0:stop] = v
                    if r1 < n:
                        vh, vl = split2(v[:, B:])
                        lh, ll = vh[:, : n - r1], vl[:, : n - r1]
                        work[s, r1:, r1:stop] -= lax.dot_general(
                            jnp.concatenate([lh, lh, ll], axis=0),
                            jnp.concatenate([vh, vl, vh], axis=0),
                            (((0,), (0,)), ((), ())),
                            preferred_element_type=F32,
                        )

        return 0

    lax.fori_loop(begin, end, body, 0)


def place_of():
    scen, crow, ccol = (lax.axis_index(a) for a in ("scen", "crow", "ccol"))
    return scen // 2, scen % 2, crow // 2, crow % 2, ccol


def device(x, z, core, y):
    return (x * 2 + z // 2, z % 2 * 2 + core, y)


class Copies:
    def __init__(self, send, recv):
        self.send, self.recv, self.used = send, recv, 0

    def start(self, src, dst, other):
        k = self.used
        self.used += 1
        copy = pltpu.make_async_remote_copy(
            src_ref=src,
            dst_ref=dst,
            send_sem=self.send.at[k],
            recv_sem=self.recv.at[k],
            device_id=other,
            device_id_type=MESH,
        )
        copy.start()
        return copy


COPIES = 96


def at(start, size, step):
    return pl.ds(pl.multiple_of(start, step), size)


def second_step(work, tri, step, out):
    S, n, _ = work.shape
    panel = step.shape[1]
    f = step[...]
    moved = [
        work[s, :, n + panel + panel // 2 : n + panel + panel // 2 + 1]
        - jnp.sum(work[s, :, n : n + panel] * f, axis=1, keepdims=True)
        for s in range(S)
    ]
    x = [[None] * (n // B) for _ in range(S)]
    for j in reversed(range(n // B)):
        rows = slice(j * B, (j + 1) * B)
        for s in range(S):
            left = moved[s][rows]
            for i in range(j + 1, n // B):
                left = left - jnp.sum(
                    work[s, rows, i * B : (i + 1) * B] * x[s][i], axis=1, keepdims=True
                )
            x[s][j] = jnp.sum(tri[s, j] * left, axis=0, keepdims=True)
            out[s : s + 1, j * B : (j + 1) * B] = x[s][j]


def whole_kernel(
    kkt, border, linked, rhs_second, diag, rhs,
    out, step, second,
    work, tri_s, blk_s,
    y, y_all, ids, ids_all, y_cut,
    head, got_core, acc, got_x, acc_x, got_yz, total,
    dense, far_rows, x_first, z_first, got_a, got_b, half_a, half_b, got_c, got_d, chunk, rows,
    head_work, tri, blk, send, recv, load,
):
    S, n, _ = kkt.shape
    x, z_hi, z_lo, core, c = place_of()
    z = z_hi * 2 + z_lo
    scen = x * 2 + z_hi
    num_cols, links, cols = y.shape
    half = links // S
    panel = num_cols * cols
    block = far_rows.shape[1]
    size = chunk.shape[0]

    sibling = device(x, z, 1 - core, c)
    x_others = [device((x + p) % 4, z, core, c) for p in range(1, 4)]
    g = z * num_cols + c
    group = 4 * num_cols
    yz_index = [(g + p) % group for p in range(1, group)]
    yz_others = [device(x, o // num_cols, core, o % num_cols) for o in yz_index]
    z_others = [device(x, (z + p) % 4, core, c) for p in range(1, 4)]
    both_others = [device((x + p) % 4, (z + 2) % 4, core, c) for p in range(1, 4)]
    c_index = [(c + p) % num_cols for p in (1, 3, 2)]
    c_others = [device(x, z, core, o) for o in c_index]
    c_from = [(c + num_cols - p) % num_cols for p in (1, 3, 2)]
    barrier = pltpu.get_barrier_semaphore()
    greeted = [sibling] + x_others + yz_others + both_others
    for other in greeted:
        pl.semaphore_signal(barrier, inc=1, device_id=other, device_id_type=MESH)
    copies = Copies(send, recv)

    loads = [pltpu.make_async_copy(kkt.at[s], work.at[s, :, :n], load.at[s]) for s in range(S)]
    for m in loads:
        m.start()
    lanes = lax.broadcasted_iota(jnp.int32, (n, panel + half), 1)
    first_lane = lax.broadcasted_iota(jnp.int32, (n, B), 1) == 0
    links_t = jnp.concatenate([linked[...]] * (8 // S), axis=0).T
    rhs_t = jnp.concatenate([rhs_second[...]] * (8 // S), axis=0).T
    for s in range(S):
        own = links_t[:, s : s + 1]
        before = jnp.where(linked[s : s + 1, :] < own, 1.0, 0.0)
        rank = jnp.sum(before, axis=1, keepdims=True).astype(jnp.int32)
        place = jnp.where(own < panel, own, panel + rank - (n - half))
        hot = jnp.where(lanes == place, 1.0, 0.0)
        row_ids = jnp.sum(jnp.where(lanes[:, panel:] == place, own, 0), axis=0, keepdims=True)
        for q in range(half // B):
            k = s * (half // B) + q
            ids[k : k + 1, :] = row_ids[:, q * B : (q + 1) * B]
        work[s, :, n : n + panel + half] = jnp.dot(
            border[s], hot.astype(BF16), preferred_element_type=F32
        )
        work[s, :, n + panel + half :] = jnp.where(first_lane, rhs_t[:, s : s + 1], 0.0)
    for m in loads:
        m.wait()
    factor(work, blk_s, tri_s, 0, n // B, False)

    pl.semaphore_wait(barrier, len(greeted))
    from_c = [[copies.start(ids, ids_all.at[c], other)] for other in c_others]
    for s in range(S):
        wp = work[s, :, n : n + panel]
        wo = work[s, :, n + panel : n + panel + half]
        pair = dot_t(wo, wp)
        for o in range(num_cols):
            y[o, s * half : (s + 1) * half] = pair[:, o * cols : (o + 1) * cols]
        span = pl.ds(s * half, half)
        for k in range(2):
            from_c[k].append(
                copies.start(y.at[c_index[k], span], y_all.at[c, span], c_others[k])
            )
    for s in range(S):
        wp = work[s, :, n : n + panel]
        part = dot_t(wp, wp)
        head[...] = part if s == 0 else head[...] + part

    base = lax.broadcasted_iota(jnp.int32, (block, B), 0)

    def place_rows(source, blocks, first):
        def body(k, _):
            r0 = (k * 2 + blocks) * block
            where = [
                jnp.where(base + r0 == ids_all[source, q : q + 1, :], 1.0, 0.0).astype(BF16)
                for q in range(links // B)
            ]
            put = jnp.dot(jnp.concatenate(where, axis=1), y_cut[...], preferred_element_type=F32)
            put = put[:, :cols] + put[:, cols:]
            to = at(r0, block, block)
            dense[to, :] = put if first else dense[to, :] + put
            return 0

        lax.fori_loop(0, 2, body, 0)

    def cut(source):
        hi, lo = split2(y_all[source])
        y_cut[:, :cols] = hi
        y_cut[:, cols:] = lo

    def place(k):
        for m in from_c[k]:
            m.wait()
        cut(c_from[k])
        place_rows(c_from[k], 1 - core, False)

    wide = n // 2
    own_l = at(core * wide, wide, wide)
    far_l = at((1 - core) * wide, wide, wide)
    pair = copies.start(head.at[:, far_l], got_core, sibling)
    from_c[2].append(copies.start(y.at[c_index[2]], y_all.at[c], c_others[2]))
    ids_all[c] = ids[...]
    y_all[c] = y[c]
    cut(c)
    place_rows(c, 1 - core, True)
    pair.wait()
    acc[...] = head[:, own_l] + got_core[...]
    rows_x = n // 4
    moves = [
        copies.start(acc.at[at((x + p) % 4 * rows_x, rows_x, rows_x), :], got_x.at[p - 1], other)
        for p, other in zip(range(1, 4), x_others)
    ]
    place_rows(c, core, True)
    place(0)
    place_rows(c_from[0], core, False)
    for m in moves:
        m.wait()
    mine = at(x * rows_x, rows_x, rows_x)
    acc_x[...] = acc[mine, :] + got_x[0] + got_x[1] + got_x[2]
    moves = [
        copies.start(acc_x.at[at(o * 8, 8, 8), :], got_yz.at[p], other)
        for p, (o, other) in enumerate(zip(yz_index, yz_others))
    ]
    place(1)
    place_rows(c_from[1], core, False)
    for m in moves:
        m.wait()
    tile = acc_x[at(g * 8, 8, 8), :]
    for p in range(group - 1):
        tile = tile + got_yz[p]
    spot = at(x * rows_x + g * 8, 8, 8)
    total[spot, own_l] = tile
    moves = [copies.start(total.at[spot, own_l], total.at[spot, own_l], o) for o in yz_others]
    place(2)
    fars = [
        copies.start(dense.at[at((k * 2 + 1 - core) * block, block, block), :], far_rows.at[k], sibling)
        for k in range(2)
    ]
    place_rows(c_from[2], core, False)
    for m in moves:
        m.wait()
    moves = [copies.start(total.at[mine, own_l], total.at[mine, own_l], o) for o in x_others]

    piece = size // 2
    for k in range(2):
        fars[k].wait()
        for d in range(8):
            to_x, to_z = d // 2, d % 2 * 2 + k
            r0 = d * size
            from_own = (k * 2 + core) * block + r0
            x_first[to_x, to_z] = dense[at(from_own, piece, piece), :] + far_rows[k, r0 : r0 + piece]
            r0 += piece
            z_first[to_z, to_x] = (
                dense[at(from_own + piece, piece, piece), :] + far_rows[k, r0 : r0 + piece]
            )
    steps = []
    for p in range(1, 4):
        steps.append(copies.start(x_first.at[(x + p) % 4], got_a.at[p - 1], x_others[p - 1]))
        steps.append(copies.start(z_first.at[(z + p) % 4], got_b.at[p - 1], z_others[p - 1]))
    for m in moves:
        m.wait()
    pair = copies.start(total.at[:, own_l], total.at[:, own_l], sibling)
    pair.wait()

    r_i = lax.broadcasted_iota(jnp.int32, (n, n), 0)
    c_i = lax.broadcasted_iota(jnp.int32, (n, n), 1)
    head_work[0, :, :n] = total[...] + jnp.where(r_i == c_i, diag[...], 0.0)
    head_work[0, :, n : 2 * n] = jnp.where(r_i == c_i, 1.0, 0.0)
    factor(head_work, blk, tri, 0, n // B - 2, True)

    for m in steps:
        m.wait()
    half_a[...] = x_first[x] + got_a[0] + got_a[1] + got_a[2]
    half_b[...] = z_first[z] + got_b[0] + got_b[1] + got_b[2]
    steps = []
    for p in range(1, 4):
        steps.append(copies.start(half_a.at[(z + p) % 4], got_c.at[p - 1], z_others[p - 1]))
        steps.append(copies.start(half_b.at[(x + p) % 4], got_d.at[p - 1], x_others[p - 1]))
    factor(head_work, blk, tri, n // B - 2, n // B - 1, True)
    for m in steps:
        m.wait()
    chunk[:piece] = half_a[z] + got_c[0] + got_c[1] + got_c[2]
    chunk[piece:] = half_b[x] + got_d[0] + got_d[1] + got_d[2]
    moves = [copies.start(chunk, rows.at[c], other) for other in c_others]
    rows[c] = chunk[...]
    factor(head_work, blk, tri, n // B - 1, n // B, True)
    for m in moves:
        m.wait()

    own_c = at(c * cols, cols, cols)
    lower = None
    for k in range(num_cols):
        term = dot_nt(rows[k], head_work[0, own_c, n + k * cols : n + (k + 1) * cols])
        lower = term if lower is None else lower + term
    top_at = at(scen % 2 * size, size, size)
    r_s = lax.broadcasted_iota(jnp.int32, (cols, size), 0) + c * cols
    c_s = lax.broadcasted_iota(jnp.int32, (cols, size), 1) + scen % 2 * size
    top = jnp.where(c_s >= r_s, head_work[0, own_c, top_at], 0.0).T
    is_top = (z_lo * 2 + core == 0) & (scen * size < n)
    slot = at(scen * size, size, size)
    out[slot, :] = jnp.where(is_top, top, lower)
    moves = [
        copies.start(out.at[slot, :], out.at[slot, :], ((scen + p) % 8, z_lo * 2 + core, c))
        for p in range(1, 8)
    ]
    inverse = head_work[0, :, n:]
    inner = jnp.sum(inverse * rhs[...], axis=1, keepdims=True)
    step[...] = jnp.sum(inverse * inner, axis=0, keepdims=True)
    second_step(work, tri_s, step, second)
    for m in moves:
        m.wait()


VMEM = pl.BlockSpec(memory_space=pltpu.VMEM)
MESH = pl.DeviceIdType.MESH
LIMIT = 62 * 2**20


def shape(*dims, dtype=F32):
    return jax.ShapeDtypeStruct(dims, dtype)


def per_device(kkt, border, linked, rhs_second, rhs_first, first_diag):
    S, n, _ = kkt.shape
    panel = rhs_first.shape[0]
    num_rows = lax.axis_size("crow")
    num_cols = lax.axis_size("ccol")
    num_scen = lax.axis_size("scen")
    tile_rows = FIRST // num_rows
    cols = panel // num_cols
    half = n - INSIDE
    width = n + panel + half + B
    group = 4 * num_cols
    size = tile_rows // num_scen
    dma = pltpu.SemaphoreType.DMA
    vmem = pltpu.VMEM
    panel_factor, step, second = pl.pallas_call(
        whole_kernel,
        out_shape=(shape(tile_rows, cols), shape(1, panel), shape(S, n)),
        in_specs=[pl.BlockSpec(memory_space=pl.ANY)] + [VMEM] * 5,
        out_specs=(VMEM,) * 3,
        scratch_shapes=[
            vmem((S, n, width), F32),
            vmem((S, n // B, B, B), F32),
            vmem((S, B, B), F32),
            vmem((num_cols, S * half, cols), F32),
            vmem((num_cols, S * half, cols), F32),
            vmem((S * half // B, B), jnp.int32),
            vmem((num_cols, S * half // B, B), jnp.int32),
            vmem((S * half, 2 * cols), BF16),
            vmem((panel, panel), F32),
            vmem((panel, panel // 2), F32),
            vmem((panel, panel // 2), F32),
            vmem((3, panel // 4, panel // 2), F32),
            vmem((panel // 4, panel // 2), F32),
            vmem((group - 1, 8, panel // 2), F32),
            vmem((panel, panel), F32),
            vmem((FIRST, cols), F32),
            vmem((2, tile_rows, cols), F32),
            vmem((4, 4, size // 2, cols), F32),
            vmem((4, 4, size // 2, cols), F32),
            vmem((3, 4, size // 2, cols), F32),
            vmem((3, 4, size // 2, cols), F32),
            vmem((4, size // 2, cols), F32),
            vmem((4, size // 2, cols), F32),
            vmem((3, size // 2, cols), F32),
            vmem((3, size // 2, cols), F32),
            vmem((size, cols), F32),
            vmem((num_cols, size, cols), F32),
            vmem((1, panel, 2 * panel), F32),
            vmem((1, panel // B, B, B), F32),
            vmem((1, B, B), F32),
            dma((COPIES,)),
            dma((COPIES,)),
            dma((S,)),
        ],
        compiler_params=pltpu.CompilerParams(
            vmem_limit_bytes=LIMIT, collective_id=0, has_side_effects=True
        ),
        cost_estimate=pl.CostEstimate(flops=10**11, bytes_accessed=2**23, transcendentals=0),
    )(kkt, border, linked, rhs_second, first_diag[None, :], rhs_first[None, :])
    return (panel_factor, step[0], second)


def solution(mesh):
    placed = (
        P(("scen", "crow", "ccol"), None, None),
        P(("scen", "crow", "ccol"), None, None),
        P(("scen", "crow", "ccol"), None),
        P(("scen", "crow", "ccol"), None),
        P(),
        P(),
    )
    return jax.shard_map(
        per_device,
        mesh=mesh,
        in_specs=placed,
        out_specs=(P("crow", "ccol"), P(), P(("scen", "crow", "ccol"), None)),
        check_vma=False,
    )
```

```python
import jax
import jax.numpy as jnp
from jax import lax
from jax.experimental import pallas as pl
from jax.experimental.pallas import tpu as pltpu
from jax.sharding import PartitionSpec as P

F32 = jnp.float32
BF16 = jnp.bfloat16
B = 128
FIRST = 8192
INSIDE = 256


def split2(x):
    hi = x.astype(BF16)
    lo = (x - hi.astype(F32)).astype(BF16)
    return hi, lo


def dot_t(x, y):
    xh, xl = split2(x)
    yh, yl = split2(y)
    return lax.dot_general(
        jnp.concatenate([xh, xh, xl], axis=0),
        jnp.concatenate([yh, yl, yh], axis=0),
        (((0,), (0,)), ((), ())),
        preferred_element_type=F32,
    )


def dot_n(x, y):
    xh, xl = split2(x)
    yh, yl = split2(y)
    return lax.dot_general(
        jnp.concatenate([xh, xh, xl], axis=1),
        jnp.concatenate([yh, yl, yh], axis=0),
        (((1,), (0,)), ((), ())),
        preferred_element_type=F32,
    )


def dot_nt(x, y):
    xh, xl = split2(x)
    yh, yl = split2(y)
    return lax.dot_general(
        jnp.concatenate([xh, xh, xl], axis=1),
        jnp.concatenate([yh, yl, yh], axis=1),
        (((1,), (1,)), ((), ())),
        preferred_element_type=F32,
    )


def pieces3(x):
    h = x.astype(BF16).astype(F32)
    r = x - h
    m = r.astype(BF16).astype(F32)
    return h, m, r - m


def rank8(x, y):
    xh, xm, xl = pieces3(x)
    yh, ym, yl = pieces3(y)
    return lax.dot_general(
        jnp.concatenate([xh, xh, xm, xm, xh, xl], axis=0).astype(BF16),
        jnp.concatenate([yh, ym, yh, ym, yl, yh], axis=0).astype(BF16),
        (((0,), (0,)), ((), ())),
        preferred_element_type=F32,
    )


def eliminate_block(blk):
    S = blk.shape[0]
    lane = lax.broadcasted_iota(jnp.int32, (1, 8, B), 2)
    row = lax.broadcasted_iota(jnp.int32, (1, 8, B), 1)
    tiles = B // 8
    p = blk[:, 0:8, :]
    for t in range(tiles):
        k0 = 8 * t

        def spread(v, m):
            return jnp.broadcast_to(v[:, :, k0 + m : k0 + m + 1], (S, 8, B))

        ahead = t < tiles - 1
        q = blk[:, k0 + 8 : k0 + 16, :] if ahead else None
        cols = [spread(p, m) for m in range(8)]
        qcols = [spread(q, m) for m in range(8)] if ahead else None
        scale = jnp.zeros((S, 8, B), F32)
        for j in range(8):
            rd = jnp.broadcast_to(1.0 / cols[j][:, j : j + 1, :], (S, 8, B))
            scale = jnp.where(row == j, rd, scale)
            here = lane == k0 + j
            prow = jnp.where(here[:, :1], 1.0, p[:, j : j + 1, :])
            crow = [cols[m][:, j : j + 1, :] for m in range(8)]
            if j < 7:
                mult = jnp.where(row > j, cols[j], 0.0) * rd
                p = jnp.where(here & (row > j), 0.0, p) - mult * prow
                for m in range(j + 1, 8):
                    cols[m] = cols[m] - mult * crow[m]
            if ahead:
                mult = qcols[j] * rd
                q = jnp.where(here, 0.0, q) - mult * prow
                for m in range(j + 1, 8):
                    qcols[m] = qcols[m] - mult * crow[m]
        blk[:, k0 : k0 + 8, :] = p
        r0 = k0 + 16
        if r0 < B:
            off = lane - k0
            scaled = p * scale
            aug = jnp.where((off > row) & (off < 8), 0.0, jnp.where(off == row, 1.0, p))
            inblk = (off >= 0) & (off < 8)
            for s in range(S):
                upd = rank8(scaled[s], aug[s])
                blk[s, r0:, :] = jnp.where(inblk[0, :1], 0.0, blk[s, r0:, :]) - upd[r0:, :]
        p = q


def factor(work, blk, tri, begin, end, unit):
    S, n, width = work.shape
    steps = n // B
    r_i = lax.broadcasted_iota(jnp.int32, (B, B), 0)
    c_i = lax.broadcasted_iota(jnp.int32, (B, B), 1)

    def body(j, _):
        rows = pl.ds(pl.multiple_of(j * B, B), B)
        blk[...] = work[:, rows, rows]
        eliminate_block(blk)
        for jj in range(begin, end):

            @pl.when(j == jj)
            def _(jj=jj):
                r0 = jj * B
                r1 = r0 + B
                stop = n + r1 if unit else width
                for s in range(S):
                    a = blk[s]
                    d = jnp.sum(jnp.where(r_i == c_i, a, 0.0), axis=1, keepdims=True)
                    t = jnp.where(c_i < r_i, a, jnp.where(c_i == r_i, 1.0, 0.0)) * lax.rsqrt(d)
                    tri[s, jj] = t
                    v = dot_n(t, work[s, r0:r1, r0:stop])
                    work[s, r0:r1, r0:stop] = v
                    if r1 < n:
                        vh, vl = split2(v[:, B:])
                        lh, ll = vh[:, : n - r1], vl[:, : n - r1]
                        work[s, r1:, r1:stop] -= lax.dot_general(
                            jnp.concatenate([lh, lh, ll], axis=0),
                            jnp.concatenate([vh, vl, vh], axis=0),
                            (((0,), (0,)), ((), ())),
                            preferred_element_type=F32,
                        )

        return 0

    lax.fori_loop(begin, end, body, 0)


def place_of():
    scen, crow, ccol = (lax.axis_index(a) for a in ("scen", "crow", "ccol"))
    return scen // 2, scen % 2, crow // 2, crow % 2, ccol


def device(x, z, core, y):
    return (x * 2 + z // 2, z % 2 * 2 + core, y)


class Copies:
    def __init__(self, send, recv):
        self.send, self.recv, self.used = send, recv, 0

    def start(self, src, dst, other):
        k = self.used
        self.used += 1
        copy = pltpu.make_async_remote_copy(
            src_ref=src,
            dst_ref=dst,
            send_sem=self.send.at[k],
            recv_sem=self.recv.at[k],
            device_id=other,
            device_id_type=MESH,
        )
        copy.start()
        return copy


COPIES = 96


def at(start, size, step):
    return pl.ds(pl.multiple_of(start, step), size)


def second_step(work, tri, step, out):
    S, n, _ = work.shape
    panel = step.shape[1]
    f = step[...]
    moved = [
        work[s, :, n + panel + panel // 2 : n + panel + panel // 2 + 1]
        - jnp.sum(work[s, :, n : n + panel] * f, axis=1, keepdims=True)
        for s in range(S)
    ]
    x = [[None] * (n // B) for _ in range(S)]
    for j in reversed(range(n // B)):
        rows = slice(j * B, (j + 1) * B)
        for s in range(S):
            left = moved[s][rows]
            for i in range(j + 1, n // B):
                left = left - jnp.sum(
                    work[s, rows, i * B : (i + 1) * B] * x[s][i], axis=1, keepdims=True
                )
            x[s][j] = jnp.sum(tri[s, j] * left, axis=0, keepdims=True)
            out[s : s + 1, j * B : (j + 1) * B] = x[s][j]


def whole_kernel(
    kkt, border, linked, rhs_second, diag, rhs,
    out, step, second,
    work, tri_s, blk_s,
    y, y_all, ids, ids_all, y_cut,
    head, got_core, acc, got_x, acc_x, got_yz, total,
    y_sib, ids_sib, base, going, got_a, got_b, half_a, half_b, got_c, got_d, chunk, rows,
    head_work, tri, blk, send, recv, load,
):
    S, n, _ = kkt.shape
    x, z_hi, z_lo, core, c = place_of()
    z = z_hi * 2 + z_lo
    scen = x * 2 + z_hi
    num_cols, links, cols = y.shape
    half = links // S
    panel = num_cols * cols
    block = base.shape[1]
    size = chunk.shape[0]

    sibling = device(x, z, 1 - core, c)
    x_others = [device((x + p) % 4, z, core, c) for p in range(1, 4)]
    g = z * num_cols + c
    group = 4 * num_cols
    yz_index = [(g + p) % group for p in range(1, group)]
    yz_others = [device(x, o // num_cols, core, o % num_cols) for o in yz_index]
    z_others = [device(x, (z + p) % 4, core, c) for p in range(1, 4)]
    both_others = [device((x + p) % 4, (z + 2) % 4, core, c) for p in range(1, 4)]
    c_index = [(c + p) % num_cols for p in (1, 3, 2)]
    c_others = [device(x, z, core, o) for o in c_index]
    c_from = [(c + num_cols - p) % num_cols for p in (1, 3, 2)]
    barrier = pltpu.get_barrier_semaphore()
    greeted = [sibling] + x_others + yz_others + both_others
    for other in greeted:
        pl.semaphore_signal(barrier, inc=1, device_id=other, device_id_type=MESH)
    copies = Copies(send, recv)

    loads = [pltpu.make_async_copy(kkt.at[s], work.at[s, :, :n], load.at[s]) for s in range(S)]
    for m in loads:
        m.start()
    lanes = lax.broadcasted_iota(jnp.int32, (n, panel + half), 1)
    first_lane = lax.broadcasted_iota(jnp.int32, (n, B), 1) == 0
    links_t = jnp.concatenate([linked[...]] * (8 // S), axis=0).T
    rhs_t = jnp.concatenate([rhs_second[...]] * (8 // S), axis=0).T
    for s in range(S):
        own = links_t[:, s : s + 1]
        before = jnp.where(linked[s : s + 1, :] < own, 1.0, 0.0)
        rank = jnp.sum(before, axis=1, keepdims=True).astype(jnp.int32)
        place = jnp.where(own < panel, own, panel + rank - (n - half))
        hot = jnp.where(lanes == place, 1.0, 0.0)
        row_ids = jnp.sum(jnp.where(lanes[:, panel:] == place, own, 0), axis=0, keepdims=True)
        for q in range(half // B):
            k = s * (half // B) + q
            ids[k : k + 1, :] = row_ids[:, q * B : (q + 1) * B]
        work[s, :, n : n + panel + half] = jnp.dot(
            border[s], hot.astype(BF16), preferred_element_type=F32
        )
        work[s, :, n + panel + half :] = jnp.where(first_lane, rhs_t[:, s : s + 1], 0.0)
    for m in loads:
        m.wait()
    factor(work, blk_s, tri_s, 0, n // B, False)

    pl.semaphore_wait(barrier, len(greeted))
    from_c = [[copies.start(ids, ids_all.at[c], other)] for other in c_others]
    for s in range(S):
        wp = work[s, :, n : n + panel]
        wo = work[s, :, n + panel : n + panel + half]
        pair = dot_t(wo, wp)
        for o in range(num_cols):
            y[o, s * half : (s + 1) * half] = pair[:, o * cols : (o + 1) * cols]
        span = pl.ds(s * half, half)
        for k in range(2):
            from_c[k].append(
                copies.start(y.at[c_index[k], span], y_all.at[c, span], c_others[k])
            )
    for s in range(S):
        wp = work[s, :, n : n + panel]
        part = dot_t(wp, wp)
        head[...] = part if s == 0 else head[...] + part

    wide = n // 2
    own_l = at(core * wide, wide, wide)
    far_l = at((1 - core) * wide, wide, wide)
    pair = copies.start(head.at[:, far_l], got_core, sibling)
    from_c[2].append(copies.start(y.at[c_index[2]], y_all.at[c], c_others[2]))
    ids_all[c] = ids[...]
    y_all[c] = y[c]

    def forward(source):
        return [
            copies.start(ids_all.at[source], ids_sib.at[source], sibling),
            copies.start(y_all.at[source], y_sib.at[source], sibling),
        ]

    passed = forward(c)
    piece = size // 2
    spot = lax.broadcasted_iota(jnp.int32, (block, B), 0)
    inside, high, low = spot & (piece - 1), (spot // piece) >> 2, (spot // piece) & 3
    for k, (to_x, to_z) in enumerate(((high, low), (low, high))):
        base[k] = (
            ((to_z & 1) * 2 + core) * block + (to_x * 2 + (to_z >> 1)) * size + k * piece + inside
        )

    def cut(rows_of, source):
        hi, lo = split2(rows_of[source])
        y_cut[:, :cols] = hi
        y_cut[:, cols:] = lo

    def put_rows(ids_of, source, k, first=False):
        where = [
            jnp.where(base[k] == ids_of[source, q : q + 1, :], 1.0, 0.0).astype(BF16)
            for q in range(links // B)
        ]
        put = jnp.dot(jnp.concatenate(where, axis=1), y_cut[...], preferred_element_type=F32)
        put = (put[:, :cols] + put[:, cols:]).reshape(4, 4, piece, cols)
        going[k] = put if first else going[k] + put

    def place_all(rows_of, ids_of, source, first=False):
        cut(rows_of, source)

        def body(k, _):
            put_rows(ids_of, source, k, first)
            return 0

        lax.fori_loop(0, 2, body, 0)

    place_all(y_all, ids_all, c, True)
    pair.wait()
    acc[...] = head[:, own_l] + got_core[...]
    rows_x = n // 4
    moves = [
        copies.start(acc.at[at((x + p) % 4 * rows_x, rows_x, rows_x), :], got_x.at[p - 1], other)
        for p, other in zip(range(1, 4), x_others)
    ]
    for m in passed:
        m.wait()
    place_all(y_sib, ids_sib, c)
    for m in from_c[0]:
        m.wait()
    passed = forward(c_from[0])
    place_all(y_all, ids_all, c_from[0])
    for m in moves:
        m.wait()
    mine = at(x * rows_x, rows_x, rows_x)
    acc_x[...] = acc[mine, :] + got_x[0] + got_x[1] + got_x[2]
    moves = [
        copies.start(acc_x.at[at(o * 8, 8, 8), :], got_yz.at[p], other)
        for p, (o, other) in enumerate(zip(yz_index, yz_others))
    ]
    for m in passed:
        m.wait()
    place_all(y_sib, ids_sib, c_from[0])
    for m in from_c[1]:
        m.wait()
    passed = forward(c_from[1])
    place_all(y_all, ids_all, c_from[1])
    for m in moves:
        m.wait()
    tile = acc_x[at(g * 8, 8, 8), :]
    for p in range(group - 1):
        tile = tile + got_yz[p]
    spot = at(x * rows_x + g * 8, 8, 8)
    total[spot, own_l] = tile
    moves = [copies.start(total.at[spot, own_l], total.at[spot, own_l], o) for o in yz_others]
    for m in passed:
        m.wait()
    place_all(y_sib, ids_sib, c_from[1])
    for m in from_c[2]:
        m.wait()
    passed = forward(c_from[2])
    for m in moves:
        m.wait()
    moves = [copies.start(total.at[mine, own_l], total.at[mine, own_l], o) for o in x_others]
    place_all(y_all, ids_all, c_from[2])
    for m in passed:
        m.wait()
    cut(y_sib, c_from[2])
    steps = []
    for k, (here, others, got) in enumerate(((x, x_others, got_a), (z, z_others, got_b))):
        put_rows(ids_sib, c_from[2], k)
        for p in range(1, 4):
            steps.append(copies.start(going.at[k, (here + p) % 4], got.at[p - 1], others[p - 1]))
    for m in moves:
        m.wait()
    pair = copies.start(total.at[:, own_l], total.at[:, own_l], sibling)
    pair.wait()

    r_i = lax.broadcasted_iota(jnp.int32, (n, n), 0)
    c_i = lax.broadcasted_iota(jnp.int32, (n, n), 1)
    head_work[0, :, :n] = total[...] + jnp.where(r_i == c_i, diag[...], 0.0)
    head_work[0, :, n : 2 * n] = jnp.where(r_i == c_i, 1.0, 0.0)
    factor(head_work, blk, tri, 0, n // B - 2, True)

    for m in steps:
        m.wait()
    half_a[...] = going[0, x] + got_a[0] + got_a[1] + got_a[2]
    half_b[...] = going[1, z] + got_b[0] + got_b[1] + got_b[2]
    steps = []
    for p in range(1, 4):
        steps.append(copies.start(half_a.at[(z + p) % 4], got_c.at[p - 1], z_others[p - 1]))
        steps.append(copies.start(half_b.at[(x + p) % 4], got_d.at[p - 1], x_others[p - 1]))
    factor(head_work, blk, tri, n // B - 2, n // B - 1, True)
    for m in steps:
        m.wait()
    chunk[:piece] = half_a[z] + got_c[0] + got_c[1] + got_c[2]
    chunk[piece:] = half_b[x] + got_d[0] + got_d[1] + got_d[2]
    moves = [copies.start(chunk, rows.at[c], other) for other in c_others]
    rows[c] = chunk[...]
    factor(head_work, blk, tri, n // B - 1, n // B, True)
    for m in moves:
        m.wait()

    own_c = at(c * cols, cols, cols)
    lower = None
    for k in range(num_cols):
        term = dot_nt(rows[k], head_work[0, own_c, n + k * cols : n + (k + 1) * cols])
        lower = term if lower is None else lower + term
    top_at = at(scen % 2 * size, size, size)
    r_s = lax.broadcasted_iota(jnp.int32, (cols, size), 0) + c * cols
    c_s = lax.broadcasted_iota(jnp.int32, (cols, size), 1) + scen % 2 * size
    top = jnp.where(c_s >= r_s, head_work[0, own_c, top_at], 0.0).T
    is_top = (z_lo * 2 + core == 0) & (scen * size < n)
    slot = at(scen * size, size, size)
    out[slot, :] = jnp.where(is_top, top, lower)
    moves = [
        copies.start(out.at[slot, :], out.at[slot, :], ((scen + p) % 8, z_lo * 2 + core, c))
        for p in range(1, 8)
    ]
    inverse = head_work[0, :, n:]
    inner = jnp.sum(inverse * rhs[...], axis=1, keepdims=True)
    step[...] = jnp.sum(inverse * inner, axis=0, keepdims=True)
    second_step(work, tri_s, step, second)
    for m in moves:
        m.wait()


VMEM = pl.BlockSpec(memory_space=pltpu.VMEM)
MESH = pl.DeviceIdType.MESH
LIMIT = 62 * 2**20


def shape(*dims, dtype=F32):
    return jax.ShapeDtypeStruct(dims, dtype)


def per_device(kkt, border, linked, rhs_second, rhs_first, first_diag):
    S, n, _ = kkt.shape
    panel = rhs_first.shape[0]
    num_rows = lax.axis_size("crow")
    num_cols = lax.axis_size("ccol")
    num_scen = lax.axis_size("scen")
    tile_rows = FIRST // num_rows
    cols = panel // num_cols
    half = n - INSIDE
    width = n + panel + half + B
    group = 4 * num_cols
    size = tile_rows // num_scen
    dma = pltpu.SemaphoreType.DMA
    vmem = pltpu.VMEM
    panel_factor, step, second = pl.pallas_call(
        whole_kernel,
        out_shape=(shape(tile_rows, cols), shape(1, panel), shape(S, n)),
        in_specs=[pl.BlockSpec(memory_space=pl.ANY)] + [VMEM] * 5,
        out_specs=(VMEM,) * 3,
        scratch_shapes=[
            vmem((S, n, width), F32),
            vmem((S, n // B, B, B), F32),
            vmem((S, B, B), F32),
            vmem((num_cols, S * half, cols), F32),
            vmem((num_cols, S * half, cols), F32),
            vmem((S * half // B, B), jnp.int32),
            vmem((num_cols, S * half // B, B), jnp.int32),
            vmem((S * half, 2 * cols), BF16),
            vmem((panel, panel), F32),
            vmem((panel, panel // 2), F32),
            vmem((panel, panel // 2), F32),
            vmem((3, panel // 4, panel // 2), F32),
            vmem((panel // 4, panel // 2), F32),
            vmem((group - 1, 8, panel // 2), F32),
            vmem((panel, panel), F32),
            vmem((num_cols, S * half, cols), F32),
            vmem((num_cols, S * half // B, B), jnp.int32),
            vmem((2, tile_rows, B), jnp.int32),
            vmem((2, 4, 4, size // 2, cols), F32),
            vmem((3, 4, size // 2, cols), F32),
            vmem((3, 4, size // 2, cols), F32),
            vmem((4, size // 2, cols), F32),
            vmem((4, size // 2, cols), F32),
            vmem((3, size // 2, cols), F32),
            vmem((3, size // 2, cols), F32),
            vmem((size, cols), F32),
            vmem((num_cols, size, cols), F32),
            vmem((1, panel, 2 * panel), F32),
            vmem((1, panel // B, B, B), F32),
            vmem((1, B, B), F32),
            dma((COPIES,)),
            dma((COPIES,)),
            dma((S,)),
        ],
        compiler_params=pltpu.CompilerParams(
            vmem_limit_bytes=LIMIT, collective_id=0, has_side_effects=True
        ),
        cost_estimate=pl.CostEstimate(flops=10**11, bytes_accessed=2**23, transcendentals=0),
    )(kkt, border, linked, rhs_second, first_diag[None, :], rhs_first[None, :])
    return (panel_factor, step[0], second)


def solution(mesh):
    placed = (
        P(("scen", "crow", "ccol"), None, None),
        P(("scen", "crow", "ccol"), None, None),
        P(("scen", "crow", "ccol"), None),
        P(("scen", "crow", "ccol"), None),
        P(),
        P(),
    )
    return jax.shard_map(
        per_device,
        mesh=mesh,
        in_specs=placed,
        out_specs=(P("crow", "ccol"), P(), P(("scen", "crow", "ccol"), None)),
        check_vma=False,
    )
```

```python
import jax
import jax.numpy as jnp
from jax import lax
from jax.experimental import pallas as pl
from jax.experimental.pallas import tpu as pltpu
from jax.sharding import PartitionSpec as P

F32 = jnp.float32
BF16 = jnp.bfloat16
B = 128
FIRST = 8192
INSIDE = 256


def split2(x):
    hi = x.astype(BF16)
    lo = (x - hi.astype(F32)).astype(BF16)
    return hi, lo


def dot_t(x, y):
    xh, xl = split2(x)
    yh, yl = split2(y)
    return lax.dot_general(
        jnp.concatenate([xh, xh, xl], axis=0),
        jnp.concatenate([yh, yl, yh], axis=0),
        (((0,), (0,)), ((), ())),
        preferred_element_type=F32,
    )


def dot_n(x, y):
    xh, xl = split2(x)
    yh, yl = split2(y)
    return lax.dot_general(
        jnp.concatenate([xh, xh, xl], axis=1),
        jnp.concatenate([yh, yl, yh], axis=0),
        (((1,), (0,)), ((), ())),
        preferred_element_type=F32,
    )


def dot_nt(x, y):
    xh, xl = split2(x)
    yh, yl = split2(y)
    return lax.dot_general(
        jnp.concatenate([xh, xh, xl], axis=1),
        jnp.concatenate([yh, yl, yh], axis=1),
        (((1,), (1,)), ((), ())),
        preferred_element_type=F32,
    )


def pieces3(x):
    h = x.astype(BF16).astype(F32)
    r = x - h
    m = r.astype(BF16).astype(F32)
    return h, m, r - m


def rank8(x, y):
    xh, xm, xl = pieces3(x)
    yh, ym, yl = pieces3(y)
    return lax.dot_general(
        jnp.concatenate([xh, xh, xm, xm, xh, xl], axis=0).astype(BF16),
        jnp.concatenate([yh, ym, yh, ym, yl, yh], axis=0).astype(BF16),
        (((0,), (0,)), ((), ())),
        preferred_element_type=F32,
    )


def eliminate_block(blk, depth):
    S = blk.shape[0]
    lane = lax.broadcasted_iota(jnp.int32, (1, 8, B), 2)
    row = lax.broadcasted_iota(jnp.int32, (1, 8, B), 1)
    tiles = B // 8
    ready = [blk[:, 8 * t : 8 * t + 8, :] for t in range(depth)]
    for t in range(tiles):
        k0 = 8 * t

        def spread(v, m):
            return jnp.broadcast_to(v[:, :, k0 + m : k0 + m + 1], (S, 8, B))

        p, ahead = ready[0], ready[1:]
        if t + depth < tiles:
            ahead.append(blk[:, k0 + 8 * depth : k0 + 8 * depth + 8, :])
        cols = [spread(p, m) for m in range(8)]
        beside = [[spread(q, m) for m in range(8)] for q in ahead]
        scale = jnp.zeros((S, 8, B), F32)
        for j in range(8):
            rd = jnp.broadcast_to(1.0 / cols[j][:, j : j + 1, :], (S, 8, B))
            scale = jnp.where(row == j, rd, scale)
            here = lane == k0 + j
            prow = jnp.where(here[:, :1], 1.0, p[:, j : j + 1, :])
            crow = [cols[m][:, j : j + 1, :] for m in range(8)]
            if j < 7:
                mult = jnp.where(row > j, cols[j], 0.0) * rd
                p = jnp.where(here & (row > j), 0.0, p) - mult * prow
                for m in range(j + 1, 8):
                    cols[m] = cols[m] - mult * crow[m]
            for k, more in enumerate(beside):
                mult = more[j] * rd
                ahead[k] = jnp.where(here, 0.0, ahead[k]) - mult * prow
                for m in range(j + 1, 8):
                    more[m] = more[m] - mult * crow[m]
        blk[:, k0 : k0 + 8, :] = p
        r0 = k0 + 8 * (depth + 1)
        if r0 < B:
            off = lane - k0
            scaled = p * scale
            aug = jnp.where((off > row) & (off < 8), 0.0, jnp.where(off == row, 1.0, p))
            inblk = (off >= 0) & (off < 8)
            for s in range(S):
                upd = rank8(scaled[s], aug[s])
                blk[s, r0:, :] = jnp.where(inblk[0, :1], 0.0, blk[s, r0:, :]) - upd[r0:, :]
        ready = ahead


def factor(work, blk, tri, begin, end, unit, depth):
    S, n, width = work.shape
    steps = n // B
    r_i = lax.broadcasted_iota(jnp.int32, (B, B), 0)
    c_i = lax.broadcasted_iota(jnp.int32, (B, B), 1)

    def body(j, _):
        rows = pl.ds(pl.multiple_of(j * B, B), B)
        blk[...] = work[:, rows, rows]
        eliminate_block(blk, depth)
        for jj in range(begin, end):

            @pl.when(j == jj)
            def _(jj=jj):
                r0 = jj * B
                r1 = r0 + B
                stop = n + r1 if unit else width
                for s in range(S):
                    a = blk[s]
                    d = jnp.sum(jnp.where(r_i == c_i, a, 0.0), axis=1, keepdims=True)
                    t = jnp.where(c_i < r_i, a, jnp.where(c_i == r_i, 1.0, 0.0)) * lax.rsqrt(d)
                    tri[s, jj] = t
                    v = dot_n(t, work[s, r0:r1, r0:stop])
                    work[s, r0:r1, r0:stop] = v
                    if r1 < n:
                        vh, vl = split2(v[:, B:])
                        lh, ll = vh[:, : n - r1], vl[:, : n - r1]
                        work[s, r1:, r1:stop] -= lax.dot_general(
                            jnp.concatenate([lh, lh, ll], axis=0),
                            jnp.concatenate([vh, vl, vh], axis=0),
                            (((0,), (0,)), ((), ())),
                            preferred_element_type=F32,
                        )

        return 0

    lax.fori_loop(begin, end, body, 0)


def place_of():
    scen, crow, ccol = (lax.axis_index(a) for a in ("scen", "crow", "ccol"))
    return scen // 2, scen % 2, crow // 2, crow % 2, ccol


def device(x, z, core, y):
    return (x * 2 + z // 2, z % 2 * 2 + core, y)


class Copies:
    def __init__(self, send, recv):
        self.send, self.recv, self.used = send, recv, 0

    def start(self, src, dst, other):
        k = self.used
        self.used += 1
        copy = pltpu.make_async_remote_copy(
            src_ref=src,
            dst_ref=dst,
            send_sem=self.send.at[k],
            recv_sem=self.recv.at[k],
            device_id=other,
            device_id_type=MESH,
        )
        copy.start()
        return copy


COPIES = 96


def at(start, size, step):
    return pl.ds(pl.multiple_of(start, step), size)


def second_step(work, tri, step, out):
    S, n, _ = work.shape
    panel = step.shape[1]
    f = step[...]
    moved = [
        work[s, :, n + panel + panel // 2 : n + panel + panel // 2 + 1]
        - jnp.sum(work[s, :, n : n + panel] * f, axis=1, keepdims=True)
        for s in range(S)
    ]
    x = [[None] * (n // B) for _ in range(S)]
    for j in reversed(range(n // B)):
        rows = slice(j * B, (j + 1) * B)
        for s in range(S):
            left = moved[s][rows]
            for i in range(j + 1, n // B):
                left = left - jnp.sum(
                    work[s, rows, i * B : (i + 1) * B] * x[s][i], axis=1, keepdims=True
                )
            x[s][j] = jnp.sum(tri[s, j] * left, axis=0, keepdims=True)
            out[s : s + 1, j * B : (j + 1) * B] = x[s][j]


def whole_kernel(
    kkt, border, linked, rhs_second, diag, rhs,
    out, step, second,
    work, tri_s, blk_s,
    y, y_all, ids, ids_all, y_cut,
    head, got_core, acc, got_x, acc_x, got_yz, total,
    y_sib, ids_sib, base, going, got_a, got_b, half_a, half_b, got_c, got_d, chunk, done, rows,
    head_work, tri, blk, send, recv, load,
):
    S, n, _ = kkt.shape
    x, z_hi, z_lo, core, c = place_of()
    z = z_hi * 2 + z_lo
    scen = x * 2 + z_hi
    num_cols, links, cols = y.shape
    half = links // S
    panel = num_cols * cols
    block = base.shape[1]
    size = chunk.shape[0]

    sibling = device(x, z, 1 - core, c)
    x_others = [device((x + p) % 4, z, core, c) for p in range(1, 4)]
    g = z * num_cols + c
    group = 4 * num_cols
    yz_index = [(g + p) % group for p in range(1, group)]
    yz_others = [device(x, o // num_cols, core, o % num_cols) for o in yz_index]
    z_others = [device(x, (z + p) % 4, core, c) for p in range(1, 4)]
    both_others = [device((x + p) % 4, (z + 2) % 4, core, c) for p in range(1, 4)]
    c_index = [(c + p) % num_cols for p in (1, 3, 2)]
    c_others = [device(x, z, core, o) for o in c_index]
    c_from = [(c + num_cols - p) % num_cols for p in (1, 3, 2)]
    barrier = pltpu.get_barrier_semaphore()
    greeted = [sibling] + x_others + yz_others + both_others
    for other in greeted:
        pl.semaphore_signal(barrier, inc=1, device_id=other, device_id_type=MESH)
    copies = Copies(send, recv)

    loads = [pltpu.make_async_copy(kkt.at[s], work.at[s, :, :n], load.at[s]) for s in range(S)]
    for m in loads:
        m.start()
    lanes = lax.broadcasted_iota(jnp.int32, (n, panel + half), 1)
    first_lane = lax.broadcasted_iota(jnp.int32, (n, B), 1) == 0
    links_t = jnp.concatenate([linked[...]] * (8 // S), axis=0).T
    rhs_t = jnp.concatenate([rhs_second[...]] * (8 // S), axis=0).T
    for s in range(S):
        own = links_t[:, s : s + 1]
        before = jnp.where(linked[s : s + 1, :] < own, 1.0, 0.0)
        rank = jnp.sum(before, axis=1, keepdims=True).astype(jnp.int32)
        place = jnp.where(own < panel, own, panel + rank - (n - half))
        hot = jnp.where(lanes == place, 1.0, 0.0)
        row_ids = jnp.sum(jnp.where(lanes[:, panel:] == place, own, 0), axis=0, keepdims=True)
        for q in range(half // B):
            k = s * (half // B) + q
            ids[k : k + 1, :] = row_ids[:, q * B : (q + 1) * B]
        work[s, :, n : n + panel + half] = jnp.dot(
            border[s], hot.astype(BF16), preferred_element_type=F32
        )
        work[s, :, n + panel + half :] = jnp.where(first_lane, rhs_t[:, s : s + 1], 0.0)
    for m in loads:
        m.wait()
    factor(work, blk_s, tri_s, 0, n // B, False, 1)

    pl.semaphore_wait(barrier, len(greeted))
    from_c = [[copies.start(ids, ids_all.at[c], other)] for other in c_others]
    for s in range(S):
        wp = work[s, :, n : n + panel]
        wo = work[s, :, n + panel : n + panel + half]
        pair = dot_t(wo, wp)
        for o in range(num_cols):
            y[o, s * half : (s + 1) * half] = pair[:, o * cols : (o + 1) * cols]
        span = pl.ds(s * half, half)
        for k in range(2):
            from_c[k].append(
                copies.start(y.at[c_index[k], span], y_all.at[c, span], c_others[k])
            )
    for s in range(S):
        wp = work[s, :, n : n + panel]
        part = dot_t(wp, wp)
        head[...] = part if s == 0 else head[...] + part

    wide = n // 2
    own_l = at(core * wide, wide, wide)
    far_l = at((1 - core) * wide, wide, wide)
    pair = copies.start(head.at[:, far_l], got_core, sibling)
    from_c[2].append(copies.start(y.at[c_index[2]], y_all.at[c], c_others[2]))
    ids_all[c] = ids[...]
    y_all[c] = y[c]

    def forward(source):
        return [
            copies.start(ids_all.at[source], ids_sib.at[source], sibling),
            copies.start(y_all.at[source], y_sib.at[source], sibling),
        ]

    passed = forward(c)
    piece = size // 2
    spot = lax.broadcasted_iota(jnp.int32, (block, B), 0)
    inside, high, low = spot & (piece - 1), (spot // piece) >> 2, (spot // piece) & 3
    for k, (to_x, to_z) in enumerate(((high, low), (low, high))):
        base[k] = (
            ((to_z & 1) * 2 + core) * block + (to_x * 2 + (to_z >> 1)) * size + k * piece + inside
        )

    def cut(rows_of, source):
        hi, lo = split2(rows_of[source])
        y_cut[:, :cols] = hi
        y_cut[:, cols:] = lo

    def put_rows(ids_of, source, k, first=False):
        where = [
            jnp.where(base[k] == ids_of[source, q : q + 1, :], 1.0, 0.0).astype(BF16)
            for q in range(links // B)
        ]
        put = jnp.dot(jnp.concatenate(where, axis=1), y_cut[...], preferred_element_type=F32)
        put = (put[:, :cols] + put[:, cols:]).reshape(4, 4, piece, cols)
        going[k] = put if first else going[k] + put

    def place_all(rows_of, ids_of, source, first=False):
        cut(rows_of, source)

        def body(k, _):
            put_rows(ids_of, source, k, first)
            return 0

        lax.fori_loop(0, 2, body, 0)

    place_all(y_all, ids_all, c, True)
    pair.wait()
    acc[...] = head[:, own_l] + got_core[...]
    rows_x = n // 4
    moves = [
        copies.start(acc.at[at((x + p) % 4 * rows_x, rows_x, rows_x), :], got_x.at[p - 1], other)
        for p, other in zip(range(1, 4), x_others)
    ]
    for m in passed:
        m.wait()
    place_all(y_sib, ids_sib, c)
    for m in from_c[0]:
        m.wait()
    passed = forward(c_from[0])
    place_all(y_all, ids_all, c_from[0])
    for m in moves:
        m.wait()
    mine = at(x * rows_x, rows_x, rows_x)
    acc_x[...] = acc[mine, :] + got_x[0] + got_x[1] + got_x[2]
    moves = [
        copies.start(acc_x.at[at(o * 8, 8, 8), :], got_yz.at[p], other)
        for p, (o, other) in enumerate(zip(yz_index, yz_others))
    ]
    for m in passed:
        m.wait()
    place_all(y_sib, ids_sib, c_from[0])
    for m in from_c[1]:
        m.wait()
    passed = forward(c_from[1])
    place_all(y_all, ids_all, c_from[1])
    for m in moves:
        m.wait()
    tile = acc_x[at(g * 8, 8, 8), :]
    for p in range(group - 1):
        tile = tile + got_yz[p]
    spot = at(x * rows_x + g * 8, 8, 8)
    total[spot, own_l] = tile
    moves = [copies.start(total.at[spot, own_l], total.at[spot, own_l], o) for o in yz_others]
    for m in passed:
        m.wait()
    place_all(y_sib, ids_sib, c_from[1])
    for m in from_c[2]:
        m.wait()
    passed = forward(c_from[2])
    for m in moves:
        m.wait()
    moves = [copies.start(total.at[mine, own_l], total.at[mine, own_l], o) for o in x_others]
    place_all(y_all, ids_all, c_from[2])
    for m in passed:
        m.wait()
    cut(y_sib, c_from[2])
    steps = []
    for k, (here, others, got) in enumerate(((x, x_others, got_a), (z, z_others, got_b))):
        put_rows(ids_sib, c_from[2], k)
        for p in range(1, 4):
            steps.append(copies.start(going.at[k, (here + p) % 4], got.at[p - 1], others[p - 1]))
    for m in moves:
        m.wait()
    pair = copies.start(total.at[:, own_l], total.at[:, own_l], sibling)
    pair.wait()

    r_i = lax.broadcasted_iota(jnp.int32, (n, n), 0)
    c_i = lax.broadcasted_iota(jnp.int32, (n, n), 1)
    head_work[0, :, :n] = total[...] + jnp.where(r_i == c_i, diag[...], 0.0)
    head_work[0, :, n : 2 * n] = jnp.where(r_i == c_i, 1.0, 0.0)
    factor(head_work, blk, tri, 0, n // B - 2, True, 2)

    for m in steps:
        m.wait()
    half_a[...] = going[0, x] + got_a[0] + got_a[1] + got_a[2]
    half_b[...] = going[1, z] + got_b[0] + got_b[1] + got_b[2]
    steps = []
    for p in range(1, 4):
        steps.append(copies.start(half_a.at[(z + p) % 4], got_c.at[p - 1], z_others[p - 1]))
        steps.append(copies.start(half_b.at[(x + p) % 4], got_d.at[p - 1], x_others[p - 1]))
    factor(head_work, blk, tri, n // B - 2, n // B - 1, True, 2)
    for m in steps:
        m.wait()
    chunk[:piece] = half_a[z] + got_c[0] + got_c[1] + got_c[2]
    chunk[piece:] = half_b[x] + got_d[0] + got_d[1] + got_d[2]
    moves = [copies.start(chunk, rows.at[c], other) for other in c_others]
    rows[c] = chunk[...]
    factor(head_work, blk, tri, n // B - 1, n // B, True, 2)
    own_c = at(c * cols, cols, cols)
    top_at = at(scen % 2 * size, size, size)
    r_s = lax.broadcasted_iota(jnp.int32, (cols, size), 0) + c * cols
    c_s = lax.broadcasted_iota(jnp.int32, (cols, size), 1) + scen % 2 * size
    top = jnp.where(c_s >= r_s, head_work[0, own_c, top_at], 0.0).T
    is_top = (z_lo * 2 + core == 0) & (scen * size < n)

    def product(source):
        return dot_nt(rows[source], head_work[0, own_c, at(n + source * cols, cols, cols)])

    done[...] = product(c)
    for m, source in zip(moves, c_from):
        m.wait()
        done[...] += product(source)
    done[...] = jnp.where(is_top, top, done[...])
    slot = at(scen * size, size, size)
    moves = [
        copies.start(done, out.at[slot, :], ((scen + p) % 8, z_lo * 2 + core, c))
        for p in range(1, 8)
    ]
    keep = pltpu.make_async_copy(done, out.at[slot, :], load.at[0])
    keep.start()
    inverse = head_work[0, :, n:]
    inner = jnp.sum(inverse * rhs[...], axis=1, keepdims=True)
    step[...] = jnp.sum(inverse * inner, axis=0, keepdims=True)
    second_step(work, tri_s, step, second)
    keep.wait()
    for m in moves:
        m.wait()


VMEM = pl.BlockSpec(memory_space=pltpu.VMEM)
MESH = pl.DeviceIdType.MESH
LIMIT = 62 * 2**20


def shape(*dims, dtype=F32):
    return jax.ShapeDtypeStruct(dims, dtype)


def per_device(kkt, border, linked, rhs_second, rhs_first, first_diag):
    S, n, _ = kkt.shape
    panel = rhs_first.shape[0]
    num_rows = lax.axis_size("crow")
    num_cols = lax.axis_size("ccol")
    num_scen = lax.axis_size("scen")
    tile_rows = FIRST // num_rows
    cols = panel // num_cols
    half = n - INSIDE
    width = n + panel + half + B
    group = 4 * num_cols
    size = tile_rows // num_scen
    dma = pltpu.SemaphoreType.DMA
    vmem = pltpu.VMEM
    panel_factor, step, second = pl.pallas_call(
        whole_kernel,
        out_shape=(shape(tile_rows, cols), shape(1, panel), shape(S, n)),
        in_specs=[pl.BlockSpec(memory_space=pl.ANY)] + [VMEM] * 5,
        out_specs=(pl.BlockSpec(memory_space=pl.ANY), VMEM, VMEM),
        scratch_shapes=[
            vmem((S, n, width), F32),
            vmem((S, n // B, B, B), F32),
            vmem((S, B, B), F32),
            vmem((num_cols, S * half, cols), F32),
            vmem((num_cols, S * half, cols), F32),
            vmem((S * half // B, B), jnp.int32),
            vmem((num_cols, S * half // B, B), jnp.int32),
            vmem((S * half, 2 * cols), BF16),
            vmem((panel, panel), F32),
            vmem((panel, panel // 2), F32),
            vmem((panel, panel // 2), F32),
            vmem((3, panel // 4, panel // 2), F32),
            vmem((panel // 4, panel // 2), F32),
            vmem((group - 1, 8, panel // 2), F32),
            vmem((panel, panel), F32),
            vmem((num_cols, S * half, cols), F32),
            vmem((num_cols, S * half // B, B), jnp.int32),
            vmem((2, tile_rows, B), jnp.int32),
            vmem((2, 4, 4, size // 2, cols), F32),
            vmem((3, 4, size // 2, cols), F32),
            vmem((3, 4, size // 2, cols), F32),
            vmem((4, size // 2, cols), F32),
            vmem((4, size // 2, cols), F32),
            vmem((3, size // 2, cols), F32),
            vmem((3, size // 2, cols), F32),
            vmem((size, cols), F32),
            vmem((size, cols), F32),
            vmem((num_cols, size, cols), F32),
            vmem((1, panel, 2 * panel), F32),
            vmem((1, panel // B, B, B), F32),
            vmem((1, B, B), F32),
            dma((COPIES,)),
            dma((COPIES,)),
            dma((S,)),
        ],
        compiler_params=pltpu.CompilerParams(
            vmem_limit_bytes=LIMIT, collective_id=0, has_side_effects=True
        ),
        cost_estimate=pl.CostEstimate(flops=10**11, bytes_accessed=2**23, transcendentals=0),
    )(kkt, border, linked, rhs_second, first_diag[None, :], rhs_first[None, :])
    return (panel_factor, step[0], second)


def solution(mesh):
    placed = (
        P(("scen", "crow", "ccol"), None, None),
        P(("scen", "crow", "ccol"), None, None),
        P(("scen", "crow", "ccol"), None),
        P(("scen", "crow", "ccol"), None),
        P(),
        P(),
    )
    return jax.shard_map(
        per_device,
        mesh=mesh,
        in_specs=placed,
        out_specs=(P("crow", "ccol"), P(), P(("scen", "crow", "ccol"), None)),
        check_vma=False,
    )
```
